512 devices in a mesh: dp: 64 (over y, z), feat: 8 (over x, core).
Axes of the slice: x: 4, y: 8, z: 8, core: 2. Of those that a mesh axis runs over, the one named last changes fastest.
Arguments:
- table: float32 [32768, 768], P('dp', 'feat'), may hold values from -6 to 6
- node_ids: int32 [65536], P('dp'), may hold values from 0 to 511
- tiles: int32 [512, 128, 128], P('dp'), may hold values 0 or 1
- tile_rows: int32 [512], P('dp'), may hold values from 0 to 1
- tile_cols: int32 [512], P('dp'), may hold values from 0 to 7, as said below
- tile_count: int32 [64], P('dp'), may hold values from 6 to 8, as said below
- seed_count: int32 [64], P('dp'), may hold values from 128 to 256, as said below
- w_self: float32 [768, 1024], P('feat'), may hold values from -0.21875 to 0.21875
- w_neigh: float32 [768, 1024], P('feat'), may hold values from -0.21875 to 0.21875
- bias: float32 [1024], P('feat'), may hold values from -3 to 3
- cotangent: bfloat16 [16384, 1024], P('dp', 'feat'), may hold values from -0.046875 to 0.046875
Outputs:
- hidden: bfloat16 [16384, 1024], P('dp', 'feat')
- grad_self: float32 [768, 1024], P('feat')
- grad_neigh: float32 [768, 1024], P('feat')
- grad_bias: float32 [1024], P('feat')
The draws below stay inside these ranges and needn't reach their ends.
Inputs may be any that keep to these rules, and one draw needn't show every extreme that they name: `node_ids`: entry k of a dp index's 1024 entries is a row within the block of 512 table rows held by dp index k // 16; repeats occur. `tile_rows`: tiles may share coordinates; their edges then add. `tile_cols`: each of a dp index's 6 sampled blocks past its targets is the column block of at least one of its live tiles. A dp index uses its first tile_count tiles; some index uses all 8. A dp index's first seed_count targets are live; some index has all 256.
All inputs are finite; a program needn't handle non-finite values. No bound on the sum of `tiles` on one device may be relied on, other than what follows from the above.
Results may differ from the reference program's by a relative error of at most 0.007.
Values may be sent and summed in bfloat16 or wider, within the bound.
A program may use at most 64 MiB of HBM per device.

```python
import jax
import jax.numpy as jnp
from jax import lax

F = 768
H = 1024
BLOCK = 128
T_DEV = 256
TABLE_DEV = 512
S_DEV = 1024
TILE_CAP = 8
NEIGH_BLOCKS = 6
CAP = 16
TARGETS = 16384
TABLE_ROWS = 32768
N_DP = 64


def draw_tile_count(key, part):
    key = jax.random.fold_in(key, 11)
    spread_key, chosen_key = jax.random.split(key)
    spread_counts = jax.random.randint(spread_key, (N_DP,), NEIGH_BLOCKS, TILE_CAP + 1)
    chosen = jax.random.randint(chosen_key, (), 0, N_DP)
    return jnp.where(jnp.arange(N_DP) == chosen, TILE_CAP, spread_counts).astype(jnp.int32)


def draw_tile_cols(key, part):
    key = jax.random.fold_in(key, 37)
    order_key, extra_key = jax.random.split(key)
    order_keys = jax.random.split(order_key, N_DP)
    orders = jax.vmap(lambda single: jax.random.permutation(single, NEIGH_BLOCKS))(order_keys)
    covered = orders.astype(jnp.int32) + T_DEV // BLOCK
    extra = jax.random.randint(extra_key, (N_DP, TILE_CAP - NEIGH_BLOCKS), 0, S_DEV // BLOCK)
    return jnp.concatenate([covered, extra.astype(jnp.int32)], axis=1).reshape(N_DP * TILE_CAP).astype(jnp.int32)


def draw_seed_count(key, part):
    key = jax.random.fold_in(key, 23)
    spread_key, chosen_key = jax.random.split(key)
    spread_counts = jax.random.randint(spread_key, (N_DP,), T_DEV // 2, T_DEV + 1)
    chosen = jax.random.randint(chosen_key, (), 0, N_DP)
    return jnp.where(jnp.arange(N_DP) == chosen, T_DEV, spread_counts).astype(jnp.int32)


def with_ends(values, rng, low, top_value):
    dims = values.shape
    place = [jax.random.randint(jax.random.fold_in(rng, axis), (), 0, dims[axis]) for axis in range(len(dims))]
    values = values.at[tuple(place)].set(low)
    longest = dims.index(max(dims))
    place[longest] = (place[longest] + 1) % dims[longest]
    return values.at[tuple(place)].set(top_value)


def level_of(stream_key, dims, shards, low, high):
    def one(dim, parts):
        steps = jax.random.uniform(jax.random.fold_in(jax.random.fold_in(stream_key, 6), dim), (parts,), jnp.float32, low / len(shards), high / len(shards))
        return jnp.repeat(jnp.exp(steps), dims[dim] // parts).reshape((-1,) + (1,) * (len(dims) - dim - 1))

    level = one(*shards[0])
    for cut in shards[1:]:
        level = level * one(*cut)
    return level


def centred(stream_key, extent, scale, bound, cuts=(), held_as=jnp.bfloat16):
    entries = jax.random.normal(stream_key, extent, jnp.float32) * scale
    if len(cuts) > 0:
        entries = level_of(stream_key, extent, cuts, -0.22, 0.18) * entries
    return jnp.clip(entries, min=-bound, max=bound).astype(held_as)


def setup_inputs(seed: int = 0) -> dict:
    arg_keys = jax.random.split(jax.random.key(seed), 12)
    return {
        "table": centred(arg_keys[0], (TABLE_ROWS, F), 1.0, 6.0, ((0, 64), (1, 8)), jnp.float32),
        "node_ids": with_ends(jax.random.randint(arg_keys[1], (N_DP * S_DEV,), 0, TABLE_DEV), jax.random.fold_in(arg_keys[1], 1), 0, TABLE_DEV - 1).astype(jnp.int32),
        "tiles": with_ends((jax.random.randint(arg_keys[2], (N_DP * TILE_CAP, BLOCK, BLOCK), 0, 16) < 1).astype(jnp.int32), jax.random.fold_in(arg_keys[2], 1), 0, 1),
        "tile_rows": with_ends(jax.random.randint(arg_keys[3], (N_DP * TILE_CAP,), 0, T_DEV // BLOCK), jax.random.fold_in(arg_keys[3], 1), 0, (T_DEV // BLOCK) - 1).astype(jnp.int32),
        "tile_cols": draw_tile_cols(jax.random.fold_in(arg_keys[11], 71), 0),
        "tile_count": draw_tile_count(jax.random.fold_in(arg_keys[11], 71), 0),
        "seed_count": draw_seed_count(jax.random.fold_in(arg_keys[11], 71), 0),
        "w_self": centred(arg_keys[7], (F, H), F ** -0.5, 0.21875, ((0, 8),), jnp.float32),
        "w_neigh": centred(arg_keys[8], (F, H), F ** -0.5, 0.21875, ((0, 8),), jnp.float32),
        "bias": centred(arg_keys[9], (H,), 0.5, 3.0, ((0, 8),), jnp.float32),
        "cotangent": centred(arg_keys[10], (TARGETS, H), (TARGETS ** -0.5), 0.046875, ((0, 64), (1, 8))),
    }


def reference(table, node_ids, tiles, tile_rows, tile_cols, tile_count, seed_count, w_self, w_neigh, bias, cotangent):
    highest = lax.Precision.HIGHEST
    owners = (jnp.arange(S_DEV, dtype=jnp.int32) // CAP) * TABLE_DEV

    def device_step(carry, inputs):
        asked_rows, tile_blocks, row_blocks, col_blocks, tile_total, seed_total, cotangent_rows = inputs
        sampled = table[owners + asked_rows]

        def add_tile(step, state):
            summed, degree = state
            weight_live = (step < tile_total).astype(jnp.float32)
            tile_block = tile_blocks[step].astype(jnp.float32)
            sources = lax.dynamic_slice_in_dim(sampled, col_blocks[step] * BLOCK, BLOCK, 0)
            start = row_blocks[step] * BLOCK
            product = jnp.dot(tile_block, sources, precision=highest) * weight_live
            summed = lax.dynamic_update_slice_in_dim(summed, lax.dynamic_slice_in_dim(summed, start, BLOCK, 0) + product, start, 0)
            row_sums = jnp.sum(tile_block, axis=1) * weight_live
            degree = lax.dynamic_update_slice_in_dim(degree, lax.dynamic_slice_in_dim(degree, start, BLOCK, 0) + row_sums, start, 0)
            return summed, degree

        summed, degree = lax.fori_loop(0, TILE_CAP, add_tile, (jnp.zeros((T_DEV, F), jnp.float32), jnp.zeros((T_DEV,), jnp.float32)))
        neighbour_mean = summed / jnp.maximum(degree, 1.0)[:, None]
        self_rows = sampled[:T_DEV]
        preact = jnp.dot(self_rows, w_self, precision=highest) + jnp.dot(neighbour_mean, w_neigh, precision=highest) + bias
        alive = (jnp.arange(T_DEV, dtype=jnp.int32) < seed_total).astype(jnp.float32)[:, None]
        sigma = jax.nn.sigmoid(preact)
        hidden = (preact * sigma * alive).astype(jnp.bfloat16)
        slope = (cotangent_rows.astype(jnp.float32) * alive * sigma * (1.0 + preact * (1.0 - sigma))).astype(jnp.bfloat16)
        slope_wide = slope.astype(jnp.float32)
        grad_self = carry[0] + jnp.dot(self_rows.T, slope_wide, precision=highest)
        grad_neigh = carry[1] + jnp.dot(neighbour_mean.T, slope_wide, precision=highest)
        grad_bias = carry[2] + jnp.sum(slope_wide, axis=0)
        return (grad_self, grad_neigh, grad_bias), hidden

    inputs = (node_ids.reshape(N_DP, S_DEV), tiles.reshape(N_DP, TILE_CAP, BLOCK, BLOCK), tile_rows.reshape(N_DP, TILE_CAP), tile_cols.reshape(N_DP, TILE_CAP), tile_count, seed_count, cotangent.reshape(N_DP, T_DEV, H))
    start_grads = (jnp.zeros((F, H), jnp.float32), jnp.zeros((F, H), jnp.float32), jnp.zeros((H,), jnp.float32))
    grads, hidden = lax.scan(device_step, start_grads, inputs)
    return (hidden.reshape(TARGETS, H), grads[0], grads[1], grads[2])
```

```python
import jax
import jax.numpy as jnp
from jax import lax
from jax.experimental import pallas as pl
from jax.experimental.pallas import tpu as pltpu
from jax.sharding import PartitionSpec as P

MESH = pl.DeviceIdType.MESH
F32 = jnp.float32
BF16 = jnp.bfloat16
NY, NZ, NX, NF = 8, 8, 4, 8
NDP = NY * NZ
BLK = 128
LANES = 128
TILE = 16


def dot(a, b):
    return jnp.dot(a, b, preferred_element_type=F32)


def kernel(
    table_hbm, ids_hbm, tiles_hbm, rows_s, cols_s, count_s, seed_s, ws_hbm, wn_hbm, bias_ref, cot_hbm,
    hidden_ref, gself_ref, gneigh_ref, gbias_ref,
    table_f, table_b, tiles_i, tiles_f, ws_f, wn_f, w_b, cot_v,
    ids_buf, rows_send, rows_buf, adj, x_b, xt_b,
    p_send, p_recv, p_own, sl_all,
    s1_send, s1_recv, n1_send, n1_recv, s1_own, n1_own,
    s2_send, s2_recv, n2_send, n2_recv,
    s3_buf, n3_buf, s4_buf, n4_buf,
    loc_sem, ids_ss, ids_rs, rows_ss, rows_rs, send_sem, send2_sem,
    p_rs, sl_rs, s1_rs, n1_rs, s2_rs, n2_rs, s3_rs, n3_rs, s4_rs, n4_rs,
):
    me = lax.axis_index("dp")
    feat = lax.axis_index("feat")
    y = me // NZ
    z = me % NZ
    x = feat // 2
    core = feat % 2
    fcols = table_f.shape[1]
    targets = cot_v.shape[0]
    s_tiles = s1_send.shape[1] // TILE
    n_tiles = n1_send.shape[1] // TILE

    def dp_of(yy, zz):
        return yy * NZ + zz

    own_ids = pltpu.make_async_copy(ids_hbm.at[y], ids_buf.at[me], loc_sem.at[0])
    get_table = pltpu.make_async_copy(table_hbm, table_f, loc_sem.at[1])
    get_ws = pltpu.make_async_copy(ws_hbm, ws_f, loc_sem.at[2])
    get_wn = pltpu.make_async_copy(wn_hbm, wn_f, loc_sem.at[3])
    get_tiles = pltpu.make_async_copy(tiles_hbm, tiles_i, loc_sem.at[4])
    get_cot = pltpu.make_async_copy(cot_hbm, cot_v, loc_sem.at[5])
    own_ids.start()
    get_table.start()
    get_ws.start()
    get_wn.start()
    get_tiles.start()
    get_cot.start()

    barrier = pltpu.get_barrier_semaphore()

    def greet_dp(k, c):
        pl.semaphore_signal(barrier, inc=1, device_id=((me + k) % NDP, feat), device_id_type=MESH)
        return c

    lax.fori_loop(1, NDP, greet_dp, 0)

    def greet_feat(k, c):
        pl.semaphore_signal(barrier, inc=1, device_id=(me, (feat + k) % NF), device_id_type=MESH)
        return c

    lax.fori_loop(1, NF, greet_feat, 0)
    pl.semaphore_wait(barrier, NDP - 1 + NF - 1)

    def send_ids(k, c):
        yy = (y + k // NZ) % NY
        zz = (z + k % NZ) % NZ
        pltpu.make_async_remote_copy(
            ids_hbm.at[yy], ids_buf.at[me], ids_ss, ids_rs,
            device_id=(dp_of(yy, zz), feat), device_id_type=MESH,
        ).start()
        return c

    lax.fori_loop(1, NDP, send_ids, 0)

    get_table.wait()
    table_b[...] = jnp.zeros_like(table_b)
    table_b[:, :fcols] = table_f[...].astype(BF16)
    own_ids.wait()
    pltpu.make_async_copy(ids_buf.at[pl.ds(0, NDP - 1)], ids_buf.at[pl.ds(0, NDP - 1)], ids_rs).wait()

    lane = lax.broadcasted_iota(jnp.int32, (NZ, TILE, LANES), 2)
    slot = lax.broadcasted_iota(jnp.int32, (NZ, TILE, LANES), 1)
    mine = lane == z * TILE + slot
    table_rows = table_b.shape[0]
    row_of = lax.broadcasted_iota(jnp.int32, (NZ * TILE, table_rows), 1)

    def gather(dy, c):
        yy = (y + dy) % NY
        asked = ids_buf[pl.ds(yy * NZ, NZ)].astype(F32)
        picked = jnp.where(mine, jnp.broadcast_to(asked, (NZ, TILE, LANES)), 0.0)
        column = jnp.sum(picked.reshape(NZ * TILE, LANES), axis=1, keepdims=True).astype(jnp.int32)
        hot = jnp.where(column == row_of, 1.0, 0.0).astype(BF16)
        found = dot(hot, table_b[...]).astype(BF16)
        rows_send[pl.ds(yy * NZ, NZ)] = found.reshape(NZ, TILE, LANES)
        for dz in range(NZ):
            zz = (z + dz) % NZ
            copy = pltpu.make_async_remote_copy(
                rows_send.at[dp_of(yy, zz)], rows_buf.at[me], rows_ss, rows_rs,
                device_id=(dp_of(yy, zz), feat), device_id_type=MESH,
            )
            if dz == 0:
                pl.when(dy > 0)(copy.start)
            else:
                copy.start()
        return c

    lax.fori_loop(0, NY, gather, 0)
    rows_buf[me] = rows_send[me]

    get_ws.wait()
    get_wn.wait()
    w_b[...] = jnp.zeros_like(w_b)
    for c in range(NX):
        w_b[c, :fcols] = ws_f[:, c * 256:(c + 1) * 256].astype(BF16)
        w_b[c, LANES:LANES + fcols] = wn_f[:, c * 256:(c + 1) * 256].astype(BF16)
    get_tiles.wait()
    tiles_f[...] = tiles_i[...].astype(F32)
    n_slots = tiles_f.shape[0]
    col_blocks = adj.shape[1] // BLK

    def place(i, c):
        r = i // col_blocks
        q = i % col_blocks
        total = jnp.zeros((BLK, BLK), F32)
        for k in range(n_slots):
            on = (rows_s[k] == r) & (cols_s[k] == q) & (k < count_s[0])
            total = total + tiles_f[k] * jnp.where(on, 1.0, 0.0)
        adj[pl.ds(pl.multiple_of(r * BLK, BLK), BLK), pl.ds(pl.multiple_of(q * BLK, BLK), BLK)] = total.astype(BF16)
        return c

    lax.fori_loop(0, (targets // BLK) * col_blocks, place, 0)
    degree = jnp.sum(adj[...].astype(F32), axis=1, keepdims=True)
    scale = 1.0 / jnp.maximum(degree, 1.0)
    get_cot.wait()

    pltpu.make_async_copy(rows_buf.at[pl.ds(0, NDP - 1)], rows_buf.at[pl.ds(0, NDP - 1)], rows_rs).wait()
    sampled = rows_buf[...].reshape(NDP * TILE, LANES)
    self_rows = sampled[:targets]
    neigh = dot(adj[...], sampled) * scale
    x_b[:, :LANES] = self_rows
    x_b[:, LANES:] = neigh.astype(BF16)

    def partial(k, c):
        chip = (x + 2 + k) % NX
        part = dot(x_b[...], w_b[chip])
        for co in range(2):
            p_send[chip * 2 + co] = part[:, co * LANES:(co + 1) * LANES].astype(BF16)
            to = chip * 2 + co
            copy = pltpu.make_async_remote_copy(
                p_send.at[to], p_recv.at[feat], send_sem.at[0], p_rs.at[feat],
                device_id=(me, to), device_id_type=MESH,
            )
            pl.when(to != feat)(copy.start)

            @pl.when(to == feat)
            def _():
                p_own[...] = part[:, co * LANES:(co + 1) * LANES]
        return c

    lax.fori_loop(0, NX, partial, 0)

    xs_t = self_rows.astype(F32).T
    xn_t = neigh.T
    ones = jnp.where(lax.broadcasted_iota(jnp.int32, (TILE, targets), 0) == 0, 1.0, 0.0)
    xt_b[:fcols] = xs_t[:fcols].astype(BF16)
    xt_b[fcols:fcols + TILE] = ones.astype(BF16)
    xt_b[fcols + TILE:] = xn_t[:fcols].astype(BF16)

    preact = p_own[...] + bias_ref[...]

    def add_partial(k, total):
        frm = (feat + k) % NF
        pltpu.make_async_copy(p_recv.at[frm], p_recv.at[frm], p_rs.at[frm]).wait()
        return total + p_recv[frm].astype(F32)

    preact = lax.fori_loop(1, NF, add_partial, preact)
    alive = jnp.where(lax.broadcasted_iota(jnp.int32, (targets, LANES), 0) < seed_s[0], 1.0, 0.0)
    sigma = jax.nn.sigmoid(preact)
    slope = cot_v[...].astype(F32) * alive * sigma * (1.0 + preact * (1.0 - sigma))
    sl_all[feat] = slope.astype(BF16)

    def send_slope(k, c):
        to = (feat + k) % NF
        pltpu.make_async_remote_copy(
            sl_all.at[feat], sl_all.at[feat], send_sem.at[1], sl_rs.at[feat],
            device_id=(me, to), device_id_type=MESH,
        ).start()
        return c

    lax.fori_loop(1, NF, send_slope, 0)
    hidden_ref[...] = (preact * sigma * alive).astype(BF16)

    def wait_slope(k, c):
        frm = (feat + k) % NF
        pltpu.make_async_copy(sl_all.at[frm], sl_all.at[frm], sl_rs.at[frm]).wait()
        return c

    lax.fori_loop(1, NF, wait_slope, 0)

    s_rows = s1_send.shape[1]

    def first(k, c):
        cz = (z + k) % NZ
        cy = (y + k) % NY
        g_s = dot(xt_b[:s_rows], sl_all[cz])
        g_n = dot(xt_b[s_rows:], sl_all[cy])
        s1_send[cz] = g_s.astype(BF16)
        n1_send[cy] = g_n.astype(BF16)
        pltpu.make_async_remote_copy(
            s1_send.at[cz], s1_recv.at[z], send_sem.at[2], s1_rs.at[z],
            device_id=(dp_of(y, cz), feat), device_id_type=MESH,
        ).start()
        pltpu.make_async_remote_copy(
            n1_send.at[cy], n1_recv.at[y], send_sem.at[3], n1_rs.at[y],
            device_id=(dp_of(cy, z), feat), device_id_type=MESH,
        ).start()
        return c

    lax.fori_loop(1, NZ, first, 0)
    s1_own[...] = dot(xt_b[:s_rows], sl_all[z])
    n1_own[...] = dot(xt_b[s_rows:], sl_all[y])

    def add_first(k, c):
        fz = (z + k) % NZ
        fy = (y + k) % NY
        pltpu.make_async_copy(s1_recv.at[fz], s1_recv.at[fz], s1_rs.at[fz]).wait()
        s1_own[...] += s1_recv[fz].astype(F32)
        pltpu.make_async_copy(n1_recv.at[fy], n1_recv.at[fy], n1_rs.at[fy]).wait()
        n1_own[...] += n1_recv[fy].astype(F32)
        return c

    lax.fori_loop(1, NZ, add_first, 0)
    s2_send[...] = s1_own[...].reshape(s_tiles, TILE, LANES)
    n2_send[...] = n1_own[...].reshape(n_tiles, TILE, LANES)

    def s2_copy(k):
        to = (y + k) % NY
        return to, pltpu.make_async_remote_copy(
            s2_send.at[lax.min(to, s_tiles - 1)], s2_recv.at[y], send2_sem.at[0, k], s2_rs.at[y],
            device_id=(dp_of(to, z), feat), device_id_type=MESH,
        )

    def n2_copy(k):
        to = (z + k) % NZ
        return to, pltpu.make_async_remote_copy(
            n2_send.at[lax.min(to, n_tiles - 1)], n2_recv.at[z], send2_sem.at[1, k], n2_rs.at[z],
            device_id=(dp_of(y, to), feat), device_id_type=MESH,
        )

    def second(k, c):
        to, copy = s2_copy(k)
        pl.when(to < s_tiles)(copy.start)
        to, copy = n2_copy(k)
        pl.when(to < n_tiles)(copy.start)
        return c

    lax.fori_loop(1, NZ, second, 0)

    def s3_copy(k):
        return pltpu.make_async_remote_copy(
            s3_buf.at[lax.min(y, s_tiles - 1)], s3_buf.at[lax.min(y, s_tiles - 1)], send2_sem.at[2, k], s3_rs.at[y],
            device_id=(dp_of((y + k) % NY, z), feat), device_id_type=MESH,
        )

    def n3_copy(k):
        return pltpu.make_async_remote_copy(
            n3_buf.at[lax.min(z, n_tiles - 1)], n3_buf.at[lax.min(z, n_tiles - 1)], send2_sem.at[3, k], n3_rs.at[z],
            device_id=(dp_of(y, (z + k) % NZ), feat), device_id_type=MESH,
        )

    @pl.when(y < s_tiles)
    def _():
        def add(k, total):
            frm = (y + k) % NY
            pltpu.make_async_copy(s2_recv.at[frm], s2_recv.at[frm], s2_rs.at[frm]).wait()
            return total + s2_recv[frm]

        s3_buf[lax.min(y, s_tiles - 1)] = lax.fori_loop(1, NY, add, s2_send[lax.min(y, s_tiles - 1)]).astype(BF16)

        def send(k, c):
            s3_copy(k).start()
            return c

        lax.fori_loop(1, NY, send, 0)

    @pl.when(z < n_tiles)
    def _():
        def add(k, total):
            frm = (z + k) % NZ
            pltpu.make_async_copy(n2_recv.at[frm], n2_recv.at[frm], n2_rs.at[frm]).wait()
            return total + n2_recv[frm]

        n3_buf[lax.min(z, n_tiles - 1)] = lax.fori_loop(1, NZ, add, n2_send[lax.min(z, n_tiles - 1)]).astype(BF16)

        def send(k, c):
            n3_copy(k).start()
            return c

        lax.fori_loop(1, NZ, send, 0)

    def wait_third(k, c):
        frm = (y + k) % NY
        at = lax.min(frm, s_tiles - 1)

        @pl.when(frm < s_tiles)
        def _():
            pltpu.make_async_copy(s3_buf.at[at], s3_buf.at[at], s3_rs.at[frm]).wait()

        frm2 = (z + k) % NZ
        at2 = lax.min(frm2, n_tiles - 1)

        @pl.when(frm2 < n_tiles)
        def _():
            pltpu.make_async_copy(n3_buf.at[at2], n3_buf.at[at2], n3_rs.at[frm2]).wait()

        return c

    lax.fori_loop(1, NZ, wait_third, 0)
    s4_buf[z] = s3_buf[...].reshape(s_rows, LANES)
    n4_buf[y] = n3_buf[...].reshape(n_tiles * TILE, LANES)

    def fourth(k, c):
        pltpu.make_async_remote_copy(
            s4_buf.at[z], s4_buf.at[z], send_sem.at[4], s4_rs.at[z],
            device_id=(dp_of(y, (z + k) % NZ), feat), device_id_type=MESH,
        ).start()
        pltpu.make_async_remote_copy(
            n4_buf.at[y], n4_buf.at[y], send_sem.at[5], n4_rs.at[y],
            device_id=(dp_of((y + k) % NY, z), feat), device_id_type=MESH,
        ).start()
        return c

    lax.fori_loop(1, NZ, fourth, 0)

    def wait_fourth(k, c):
        fz = (z + k) % NZ
        fy = (y + k) % NY
        pltpu.make_async_copy(s4_buf.at[fz], s4_buf.at[fz], s4_rs.at[fz]).wait()
        pltpu.make_async_copy(n4_buf.at[fy], n4_buf.at[fy], n4_rs.at[fy]).wait()
        return c

    lax.fori_loop(1, NZ, wait_fourth, 0)
    for c in range(NF):
        gself_ref[:, c * LANES:(c + 1) * LANES] = s4_buf[c][:fcols].astype(F32)
        gneigh_ref[:, c * LANES:(c + 1) * LANES] = n4_buf[c].astype(F32)
    gbias_ref[...] = s4_buf[feat][fcols:fcols + TILE].astype(F32)[:1]

    def sent(buf, count, sem):
        pltpu.make_async_copy(buf.at[pl.ds(0, count)], buf.at[pl.ds(0, count)], sem).wait()

    sent(ids_buf, NDP - 1, ids_ss)
    sent(rows_send, NDP - 1, rows_ss)
    sent(p_send, NF - 1, send_sem.at[0])
    sent(sl_all, NF - 1, send_sem.at[1])
    sent(s1_send, NZ - 1, send_sem.at[2])
    sent(n1_send, NY - 1, send_sem.at[3])
    sent(s4_buf, NZ - 1, send_sem.at[4])
    sent(n4_buf, NY - 1, send_sem.at[5])

    def left(k, c):
        to, copy = s2_copy(k)
        pl.when(to < s_tiles)(copy.wait_send)
        to, copy = n2_copy(k)
        pl.when(to < n_tiles)(copy.wait_send)
        pl.when(y < s_tiles)(s3_copy(k).wait_send)
        pl.when(z < n_tiles)(n3_copy(k).wait_send)
        return c

    lax.fori_loop(1, NZ, left, 0)


def on_device(table, node_ids, tiles, tile_rows, tile_cols, tile_count, seed_count, w_self, w_neigh, bias, cotangent):
    fcols = table.shape[1]
    hidden_all = w_self.shape[1]
    targets, hid = cotangent.shape
    s_rows, n_rows = fcols + TILE, fcols
    vmem = pltpu.VMEM
    dma = pltpu.SemaphoreType.DMA
    hbm = pl.BlockSpec(memory_space=pl.ANY)
    in_vmem = pl.BlockSpec(memory_space=pltpu.VMEM)
    smem = pl.BlockSpec(memory_space=pltpu.SMEM)
    scratch = [
        vmem(table.shape, F32),
        vmem((table.shape[0], LANES), BF16),
        vmem(tiles.shape, jnp.int32),
        vmem(tiles.shape, F32),
        vmem(w_self.shape, F32),
        vmem(w_neigh.shape, F32),
        vmem((NX, 2 * LANES, hidden_all // NX), BF16),
        vmem(cotangent.shape, BF16),
        vmem((NDP, 1, LANES), jnp.int32),
        vmem((NDP, TILE, LANES), BF16),
        vmem((NDP, TILE, LANES), BF16),
        vmem((targets, NDP * TILE), BF16),
        vmem((targets, 2 * LANES), BF16),
        vmem((s_rows + n_rows, targets), BF16),
        vmem((NF, targets, hid), BF16),
        vmem((NF, targets, hid), BF16),
        vmem((targets, hid), F32),
        vmem((NF, targets, hid), BF16),
        vmem((NZ, s_rows, LANES), BF16),
        vmem((NZ, s_rows, LANES), BF16),
        vmem((NY, n_rows, LANES), BF16),
        vmem((NY, n_rows, LANES), BF16),
        vmem((s_rows, LANES), F32),
        vmem((n_rows, LANES), F32),
        vmem((s_rows // TILE, TILE, LANES), F32),
        vmem((NY, TILE, LANES), F32),
        vmem((n_rows // TILE, TILE, LANES), F32),
        vmem((NZ, TILE, LANES), F32),
        vmem((s_rows // TILE, TILE, LANES), BF16),
        vmem((n_rows // TILE, TILE, LANES), BF16),
        vmem((NZ, s_rows, LANES), BF16),
        vmem((NY, n_rows, LANES), BF16),
        dma((6,)),
        dma, dma, dma, dma,
        dma((6,)),
        dma((4, NZ)),
    ] + [dma((8,))] * 10
    hidden, grad_self, grad_neigh, grad_bias = pl.pallas_call(
        kernel,
        out_shape=(
            jax.ShapeDtypeStruct((targets, hid), BF16),
            jax.ShapeDtypeStruct(w_self.shape, F32),
            jax.ShapeDtypeStruct(w_neigh.shape, F32),
            jax.ShapeDtypeStruct((1, hid), F32),
        ),
        in_specs=[hbm, hbm, hbm, smem, smem, smem, smem, hbm, hbm, in_vmem, hbm],
        out_specs=(in_vmem,) * 4,
        scratch_shapes=scratch,
        compiler_params=pltpu.CompilerParams(
            collective_id=0, has_side_effects=True, vmem_limit_bytes=40 * 1024 * 1024
        ),
        cost_estimate=pl.CostEstimate(flops=300_000_000, bytes_accessed=4_000_000, transcendentals=65536),
    )(
        table, node_ids.reshape(NY, 1, NZ * TILE), tiles, tile_rows, tile_cols, tile_count, seed_count,
        w_self, w_neigh, bias.reshape(1, hid), cotangent,
    )
    return hidden, grad_self, grad_neigh, grad_bias.reshape(hid)


def solution(mesh):
    placed = (
        P("dp", "feat"),
        P("dp"),
        P("dp", None, None),
        P("dp"),
        P("dp"),
        P("dp"),
        P("dp"),
        P("feat", None),
        P("feat", None),
        P("feat"),
        P("dp", "feat"),
    )
    return jax.shard_map(
        on_device,
        mesh=mesh,
        in_specs=placed,
        out_specs=(P("dp", "feat"), P("feat", None), P("feat", None), P("feat")),
        check_vma=False,
    )
```

```python
import jax
import jax.numpy as jnp
from jax import lax
from jax.experimental import pallas as pl
from jax.experimental.pallas import tpu as pltpu
from jax.sharding import PartitionSpec as P

MESH = pl.DeviceIdType.MESH
F32 = jnp.float32
BF16 = jnp.bfloat16
NY, NZ, NX, NF = 8, 8, 4, 8
NDP = NY * NZ
BLK = 128
LANES = 128
VMEM_LIMIT = 60 * 1024 * 1024
TILE = 16


RING = (4, 5, 3, 6, 2, 7, 1)
CHIPS = (2, 1, 3)


def dot(a, b):
    return jnp.dot(a, b, preferred_element_type=F32)


def dot_t(a, b):
    return lax.dot_general(a, b, (((1,), (1,)), ((), ())), preferred_element_type=F32)


def kernel(
    table_hbm, ids_hbm, tiles_hbm, rows_s, cols_s, count_s, seed_s, ws_hbm, wn_hbm, bias_ref, cot_hbm,
    hidden_ref, s4_buf, n4_buf,
    table_f, table_b, tiles_i, tiles_f, ws_f, wn_f, w_b, cot_v,
    ids_y, ids_buf, rows_send, rows_buf, adj, x_b, xt_b,
    q_send, q_recv, q_own, p_send, p_recv, sl_all,
    s1_send, s1_recv, n1_send, n1_recv, s1_own, n1_own,
    s2_send, s2_recv, n2_send, n2_recv,
    s3_buf, n3_buf,
    loc_sem, ids_ss, idy_rs, idz_rs, rows_ss, rows_rs, q_ss, q_rs, send_sem, send2_sem,
    p_rs, sl_rs, s1_rs, n1_rs, s2_rs, n2_rs, s3_rs, n3_rs, s4_rs, n4_rs,
):
    me = lax.axis_index("dp")
    feat = lax.axis_index("feat")
    y = me // NZ
    z = me % NZ
    x = feat // 2
    core = feat % 2
    fcols = table_f.shape[0]
    mate = x * 2 + 1 - core
    targets = cot_v.shape[0]
    s_tiles = s1_send.shape[1] // TILE
    n_tiles = n1_send.shape[1] // TILE

    def dp_of(yy, zz):
        return yy * NZ + zz

    own_ids = pltpu.make_async_copy(ids_hbm.at[y], ids_y.at[y], loc_sem.at[0])
    get_table = pltpu.make_async_copy(table_hbm, table_f, loc_sem.at[1])
    get_ws = pltpu.make_async_copy(ws_hbm, ws_f, loc_sem.at[2])
    get_wn = pltpu.make_async_copy(wn_hbm, wn_f, loc_sem.at[3])
    get_tiles = pltpu.make_async_copy(tiles_hbm, tiles_i, loc_sem.at[4])
    get_cot = pltpu.make_async_copy(cot_hbm, cot_v, loc_sem.at[5])
    own_ids.start()
    get_table.start()
    get_ws.start()
    get_wn.start()
    get_tiles.start()
    get_cot.start()

    barrier = pltpu.get_barrier_semaphore()

    for k in RING:
        pl.semaphore_signal(barrier, inc=1, device_id=(dp_of((y + k) % NY, z), feat), device_id_type=MESH)
    for k in RING:
        pl.semaphore_signal(barrier, inc=1, device_id=(dp_of(y, (z + k) % NZ), feat), device_id_type=MESH)
    for k in CHIPS:
        pl.semaphore_signal(barrier, inc=1, device_id=(me, (x + k) % NX * 2 + core), device_id_type=MESH)
    pl.semaphore_signal(barrier, inc=1, device_id=(me, mate), device_id_type=MESH)
    pl.semaphore_wait(barrier, NZ - 1 + NY - 1 + NX)

    for k in RING:
        yy = (y + k) % NY
        pltpu.make_async_remote_copy(
            ids_hbm.at[yy], ids_y.at[y], ids_ss.at[0], idy_rs,
            device_id=(dp_of(yy, z), feat), device_id_type=MESH,
        ).start()
    own_ids.wait()
    pltpu.make_async_copy(ids_y.at[pl.ds(0, NY - 1)], ids_y.at[pl.ds(0, NY - 1)], idy_rs).wait()
    for k in RING:
        pltpu.make_async_remote_copy(
            ids_y, ids_buf.at[z], ids_ss.at[1], idz_rs,
            device_id=(dp_of(y, (z + k) % NZ), feat), device_id_type=MESH,
        ).start()
    ids_buf[z] = ids_y[...]

    get_table.wait()
    table_b[...] = table_f[...].astype(BF16)
    pltpu.make_async_copy(ids_buf.at[pl.ds(0, NZ - 1)], ids_buf.at[pl.ds(0, NZ - 1)], idz_rs).wait()

    lane = lax.broadcasted_iota(jnp.int32, (NZ, TILE, LANES), 2)
    slot = lax.broadcasted_iota(jnp.int32, (NZ, TILE, LANES), 1)
    mine = lane == z * TILE + slot
    table_rows = table_b.shape[1]
    row_of = lax.broadcasted_iota(jnp.int32, (NZ * TILE, table_rows), 1)

    def gather(step, c):
        pair = ((y + 4 - step) % NY, (y + 5 + step) % NY)
        for yy in pair:
            asked = ids_buf[:, yy].astype(F32)
            picked = jnp.where(mine, jnp.broadcast_to(asked, (NZ, TILE, LANES)), 0.0)
            column = jnp.sum(picked.reshape(NZ * TILE, LANES), axis=1, keepdims=True).astype(jnp.int32)
            hot = jnp.where(column == row_of, 1.0, 0.0).astype(BF16)
            found = dot_t(hot, table_b[...]).astype(BF16)
            rows_send[pl.ds(yy * NZ, NZ)] = found.reshape(NZ, TILE, fcols)
        for dz in RING + (0,):
            zz = (z + dz) % NZ
            for yy in pair:
                to = dp_of(yy, zz)
                copy = pltpu.make_async_remote_copy(
                    rows_send.at[to], rows_buf.at[me], rows_ss, rows_rs,
                    device_id=(to, feat), device_id_type=MESH,
                )
                if dz == 0:
                    pl.when(to != me)(copy.start)
                else:
                    copy.start()
        return c

    lax.fori_loop(0, NY // 2, gather, 0)
    rows_buf[me] = rows_send[me]

    get_ws.wait()
    get_wn.wait()
    w_b[...] = jnp.zeros_like(w_b)
    x_b[...] = jnp.zeros_like(x_b)
    for c in range(NX):
        for co in range(2):
            at = (c * 2 + co) * LANES
            w_b[c, co, :fcols] = ws_f[:, at:at + LANES].astype(BF16)
            w_b[c, co, LANES:LANES + fcols] = wn_f[:, at:at + LANES].astype(BF16)
    get_tiles.wait()
    tiles_f[...] = tiles_i[...].astype(F32)
    n_slots = tiles_f.shape[0]
    col_blocks = adj.shape[1] // BLK

    def place(i, c):
        r = i // col_blocks
        q = i % col_blocks
        total = jnp.zeros((BLK, BLK), F32)
        for k in range(n_slots):
            on = (rows_s[k] == r) & (cols_s[k] == q) & (k < count_s[0])
            total = total + tiles_f[k] * jnp.where(on, 1.0, 0.0)
        adj[pl.ds(pl.multiple_of(r * BLK, BLK), BLK), pl.ds(pl.multiple_of(q * BLK, BLK), BLK)] = total.astype(BF16)
        return c

    lax.fori_loop(0, (targets // BLK) * col_blocks, place, 0)
    degree = jnp.sum(adj[...].astype(F32), axis=1, keepdims=True)
    scale = 1.0 / jnp.maximum(degree, 1.0)
    get_cot.wait()

    pltpu.make_async_copy(rows_buf.at[pl.ds(0, NDP - 1)], rows_buf.at[pl.ds(0, NDP - 1)], rows_rs).wait()
    sampled = rows_buf[...].reshape(NDP * TILE, fcols)
    self_rows = sampled[:targets]
    neigh = dot(adj[...], sampled) * scale
    x_b[:, :fcols] = self_rows
    x_b[:, LANES:LANES + fcols] = neigh.astype(BF16)

    def pair_copy(chip):
        return pltpu.make_async_remote_copy(
            q_send.at[chip], q_recv.at[chip], q_ss.at[chip], q_rs.at[chip],
            device_id=(me, mate), device_id_type=MESH,
        )

    for k in CHIPS + (0,):
        chip = (x + k) % NX
        q_send[chip] = dot(x_b[...], w_b[chip, 1 - core]).astype(BF16)
        pair_copy(chip).start()
    for k in CHIPS + (0,):
        chip = (x + k) % NX
        q_own[chip] = dot(x_b[...], w_b[chip, core])
    for k in CHIPS:
        chip = (x + k) % NX
        pair_copy(chip).wait_recv()
        p_send[chip] = (q_own[chip] + q_recv[chip].astype(F32)).astype(BF16)
        pltpu.make_async_remote_copy(
            p_send.at[chip], p_recv.at[x], send_sem.at[0], p_rs.at[x],
            device_id=(me, chip * 2 + core), device_id_type=MESH,
        ).start()
    pair_copy(x).wait_recv()
    preact = q_own[x] + q_recv[x].astype(F32) + bias_ref[...]

    xs_t = self_rows.astype(F32).T
    xn_t = neigh.T
    ones = jnp.where(lax.broadcasted_iota(jnp.int32, (TILE, targets), 0) == 0, 1.0, 0.0)
    xt_b[:fcols] = xs_t.astype(BF16)
    xt_b[fcols:fcols + TILE] = ones.astype(BF16)
    xt_b[fcols + TILE:] = xn_t.astype(BF16)

    for k in (1, 3, 2):
        frm = (x + k) % NX
        pltpu.make_async_copy(p_recv.at[frm], p_recv.at[frm], p_rs.at[frm]).wait()
        preact = preact + p_recv[frm].astype(F32)
    alive = jnp.where(lax.broadcasted_iota(jnp.int32, (targets, LANES), 0) < seed_s[0], 1.0, 0.0)
    sigma = jax.nn.sigmoid(preact)
    slope = cot_v[...].astype(F32) * alive * sigma * (1.0 + preact * (1.0 - sigma))
    sl_all[feat] = slope.astype(BF16)

    def slope_copy(which, sem, to):
        return pltpu.make_async_remote_copy(
            sl_all.at[which], sl_all.at[which], sem, sl_rs.at[which],
            device_id=(me, to), device_id_type=MESH,
        )

    for k in CHIPS:
        slope_copy(feat, send_sem.at[1], (x + k) % NX * 2 + core).start()
    slope_copy(feat, q_ss.at[NX], mate).start()
    hidden_ref[...] = (preact * sigma * alive).astype(BF16)

    s_rows = s1_send.shape[1]

    def first(block):
        at = block // 2 + block % 2 * NX
        g_s = dot(xt_b[:s_rows], sl_all[block])
        g_n = dot(xt_b[s_rows:], sl_all[block])

        @pl.when(at == z)
        def _():
            s1_own[...] = g_s

        @pl.when(at == y)
        def _():
            n1_own[...] = g_n

        @pl.when(at != z)
        def _():
            s1_send[at] = g_s.astype(BF16)
            pltpu.make_async_remote_copy(
                s1_send.at[at], s1_recv.at[z], send_sem.at[2], s1_rs.at[z],
                device_id=(dp_of(y, at), feat), device_id_type=MESH,
            ).start()

        @pl.when(at != y)
        def _():
            n1_send[at] = g_n.astype(BF16)
            pltpu.make_async_remote_copy(
                n1_send.at[at], n1_recv.at[y], send_sem.at[3], n1_rs.at[y],
                device_id=(dp_of(at, z), feat), device_id_type=MESH,
            ).start()

    def wait_slope(which):
        pltpu.make_async_copy(sl_all.at[which], sl_all.at[which], sl_rs.at[which]).wait()

    first(feat)
    wait_slope(mate)
    first(mate)
    for n, k in enumerate((1, 3, 2)):
        direct = (x + k) % NX * 2 + core
        passed = (x + k) % NX * 2 + 1 - core
        wait_slope(direct)
        slope_copy(direct, q_ss.at[NX + 1 + n], mate).start()
        first(direct)
        wait_slope(passed)
        first(passed)

    def add_first(own, recv, sems, here, count):
        for k in RING:
            frm = (here - k + count) % count
            pltpu.make_async_copy(recv.at[frm], recv.at[frm], sems.at[frm]).wait()
            own[...] += recv[frm].astype(F32)

    def s2_copy(k):
        to = (y + k) % NY
        return to, pltpu.make_async_remote_copy(
            s2_send.at[lax.min(to, s_tiles - 1)], s2_recv.at[y], send2_sem.at[0, k], s2_rs.at[y],
            device_id=(dp_of(to, z), feat), device_id_type=MESH,
        )

    def n2_copy(k):
        to = (z + k) % NZ
        return to, pltpu.make_async_remote_copy(
            n2_send.at[lax.min(to, n_tiles - 1)], n2_recv.at[z], send2_sem.at[1, k], n2_rs.at[z],
            device_id=(dp_of(y, to), feat), device_id_type=MESH,
        )

    def s3_copy(k):
        return pltpu.make_async_remote_copy(
            s3_buf.at[lax.min(y, s_tiles - 1)], s3_buf.at[lax.min(y, s_tiles - 1)], send2_sem.at[2, k], s3_rs.at[y],
            device_id=(dp_of((y + k) % NY, z), feat), device_id_type=MESH,
        )

    def n3_copy(k):
        return pltpu.make_async_remote_copy(
            n3_buf.at[lax.min(z, n_tiles - 1)], n3_buf.at[lax.min(z, n_tiles - 1)], send2_sem.at[3, k], n3_rs.at[z],
            device_id=(dp_of(y, (z + k) % NZ), feat), device_id_type=MESH,
        )

    add_first(s1_own, s1_recv, s1_rs, z, NZ)
    s2_send[...] = s1_own[...].reshape(s_tiles, TILE, LANES)
    for k in RING:
        to, copy = s2_copy(k)
        pl.when(to < s_tiles)(copy.start)
    add_first(n1_own, n1_recv, n1_rs, y, NY)
    n2_send[...] = n1_own[...].reshape(n_tiles, TILE, LANES)
    for k in RING:
        to, copy = n2_copy(k)
        pl.when(to < n_tiles)(copy.start)

    @pl.when(y < s_tiles)
    def _():
        total = s2_send[lax.min(y, s_tiles - 1)]
        for k in RING:
            frm = (y - k + NY) % NY
            pltpu.make_async_copy(s2_recv.at[frm], s2_recv.at[frm], s2_rs.at[frm]).wait()
            total = total + s2_recv[frm]
        s3_buf[lax.min(y, s_tiles - 1)] = total.astype(BF16)
        for k in RING:
            s3_copy(k).start()

    @pl.when(z < n_tiles)
    def _():
        total = n2_send[lax.min(z, n_tiles - 1)]
        for k in RING:
            frm = (z - k + NZ) % NZ
            pltpu.make_async_copy(n2_recv.at[frm], n2_recv.at[frm], n2_rs.at[frm]).wait()
            total = total + n2_recv[frm]
        n3_buf[lax.min(z, n_tiles - 1)] = total.astype(BF16)
        for k in RING:
            n3_copy(k).start()

    for k in RING:
        frm = (y - k + NY) % NY
        at = lax.min(frm, s_tiles - 1)
        pl.when(frm < s_tiles)(pltpu.make_async_copy(s3_buf.at[at], s3_buf.at[at], s3_rs.at[frm]).wait)
    s4_buf[z] = s3_buf[...].reshape(s_rows, LANES)
    for k in RING:
        pltpu.make_async_remote_copy(
            s4_buf.at[z], s4_buf.at[z], send_sem.at[4], s4_rs.at[z],
            device_id=(dp_of(y, (z + k) % NZ), feat), device_id_type=MESH,
        ).start()
    for k in RING:
        frm = (z - k + NZ) % NZ
        at = lax.min(frm, n_tiles - 1)
        pl.when(frm < n_tiles)(pltpu.make_async_copy(n3_buf.at[at], n3_buf.at[at], n3_rs.at[frm]).wait)
    n4_buf[y] = n3_buf[...].reshape(n_tiles * TILE, LANES)
    for k in RING:
        pltpu.make_async_remote_copy(
            n4_buf.at[y], n4_buf.at[y], send_sem.at[5], n4_rs.at[y],
            device_id=(dp_of((y + k) % NY, z), feat), device_id_type=MESH,
        ).start()
    for k in RING:
        fz = (z + k) % NZ
        fy = (y + k) % NY
        pltpu.make_async_copy(s4_buf.at[fz], s4_buf.at[fz], s4_rs.at[fz]).wait()
        pltpu.make_async_copy(n4_buf.at[fy], n4_buf.at[fy], n4_rs.at[fy]).wait()

    def sent(buf, count, sem):
        pltpu.make_async_copy(buf.at[pl.ds(0, count)], buf.at[pl.ds(0, count)], sem).wait()

    sent(ids_y, NY - 1, ids_ss.at[0])
    sent(ids_buf, NZ - 1, ids_ss.at[1])
    sent(rows_send, NDP - 1, rows_ss)
    sent(p_send, NX - 1, send_sem.at[0])
    sent(sl_all, NX - 1, send_sem.at[1])
    sent(s1_send, NZ - 1, send_sem.at[2])
    sent(n1_send, NY - 1, send_sem.at[3])
    sent(s4_buf, NZ - 1, send_sem.at[4])
    sent(n4_buf, NY - 1, send_sem.at[5])
    for c in range(NX):
        sent(q_send, 1, q_ss.at[c])
        sent(sl_all, 1, q_ss.at[NX + c])
    for k in RING:
        to, copy = s2_copy(k)
        pl.when(to < s_tiles)(copy.wait_send)
        to, copy = n2_copy(k)
        pl.when(to < n_tiles)(copy.wait_send)
        pl.when(y < s_tiles)(s3_copy(k).wait_send)
        pl.when(z < n_tiles)(n3_copy(k).wait_send)


def finish(hidden_in, s4_in, n4_in, hidden_ref, gself_ref, gneigh_ref, gbias_ref, gs_v, gn_v, gb_v, sem):
    fcols = gs_v.shape[0]
    copies = [pltpu.make_async_copy(hidden_in, hidden_ref, sem.at[0])]
    copies[0].start()
    for t in range(NF):
        c = (t % NX) * 2 + t // NX
        gs_v[:, c * LANES:(c + 1) * LANES] = s4_in[t][:fcols].astype(F32)
    copies.append(pltpu.make_async_copy(gs_v, gself_ref, sem.at[1]))
    copies[1].start()
    for t in range(NF):
        c = (t % NX) * 2 + t // NX
        gn_v[:, c * LANES:(c + 1) * LANES] = n4_in[t].astype(F32)
    copies.append(pltpu.make_async_copy(gn_v, gneigh_ref, sem.at[2]))
    copies[2].start()
    feat = lax.axis_index("feat")
    gb_v[...] = s4_in[feat // 2 + feat % 2 * NX][fcols:fcols + TILE].astype(F32)[:1]
    copies.append(pltpu.make_async_copy(gb_v, gbias_ref, sem.at[3]))
    copies[3].start()
    for copy in copies:
        copy.wait()


def on_device(table, node_ids, tiles, tile_rows, tile_cols, tile_count, seed_count, w_self, w_neigh, bias, cotangent):
    fcols = table.shape[1]
    hidden_all = w_self.shape[1]
    targets, hid = cotangent.shape
    s_rows, n_rows = fcols + TILE, fcols
    vmem = pltpu.VMEM
    dma = pltpu.SemaphoreType.DMA
    hbm = pl.BlockSpec(memory_space=pl.ANY)
    in_vmem = pl.BlockSpec(memory_space=pltpu.VMEM)
    smem = pl.BlockSpec(memory_space=pltpu.SMEM)
    scratch = [
        vmem(table.shape[::-1], F32),
        vmem(table.shape[::-1], BF16),
        vmem(tiles.shape, jnp.int32),
        vmem(tiles.shape, F32),
        vmem(w_self.shape, F32),
        vmem(w_neigh.shape, F32),
        vmem((NX, 2, 2 * LANES, LANES), BF16),
        vmem(cotangent.shape, BF16),
        vmem((NY, 1, LANES), jnp.int32),
        vmem((NZ, NY, 1, LANES), jnp.int32),
        vmem((NDP, TILE, fcols), BF16),
        vmem((NDP, TILE, fcols), BF16),
        vmem((targets, NDP * TILE), BF16),
        vmem((targets, 2 * LANES), BF16),
        vmem((s_rows + n_rows, targets), BF16),
        vmem((NX, targets, hid), BF16),
        vmem((NX, targets, hid), BF16),
        vmem((NX, targets, hid), F32),
        vmem((NX, targets, hid), BF16),
        vmem((NX, targets, hid), BF16),
        vmem((NF, targets, hid), BF16),
        vmem((NZ, s_rows, LANES), BF16),
        vmem((NZ, s_rows, LANES), BF16),
        vmem((NY, n_rows, LANES), BF16),
        vmem((NY, n_rows, LANES), BF16),
        vmem((s_rows, LANES), F32),
        vmem((n_rows, LANES), F32),
        vmem((s_rows // TILE, TILE, LANES), F32),
        vmem((NY, TILE, LANES), F32),
        vmem((n_rows // TILE, TILE, LANES), F32),
        vmem((NZ, TILE, LANES), F32),
        vmem((s_rows // TILE, TILE, LANES), BF16),
        vmem((n_rows // TILE, TILE, LANES), BF16),
        dma((6,)),
        dma((2,)), dma, dma, dma, dma,
        dma((2 * NX,)), dma((NX,)),
        dma((6,)),
        dma((4, NZ)),
    ] + [dma((8,))] * 10
    hidden, s4, n4 = pl.pallas_call(
        kernel,
        out_shape=(
            jax.ShapeDtypeStruct((targets, hid), BF16),
            jax.ShapeDtypeStruct((NZ, s_rows, LANES), BF16),
            jax.ShapeDtypeStruct((NY, n_rows, LANES), BF16),
        ),
        in_specs=[hbm, hbm, hbm, smem, smem, smem, smem, hbm, hbm, in_vmem, hbm],
        out_specs=(in_vmem,) * 3,
        scratch_shapes=scratch,
        compiler_params=pltpu.CompilerParams(
            collective_id=0, has_side_effects=True, vmem_limit_bytes=VMEM_LIMIT
        ),
        cost_estimate=pl.CostEstimate(flops=300_000_000, bytes_accessed=4_000_000, transcendentals=65536),
    )(
        table.T, node_ids.reshape(NY, 1, NZ * TILE), tiles, tile_rows, tile_cols,
        tile_count, seed_count, w_self, w_neigh, bias.reshape(1, hid), cotangent,
    )
    hidden, grad_self, grad_neigh, grad_bias = pl.pallas_call(
        finish,
        out_shape=(
            jax.ShapeDtypeStruct((targets, hid), BF16),
            jax.ShapeDtypeStruct(w_self.shape, F32),
            jax.ShapeDtypeStruct(w_neigh.shape, F32),
            jax.ShapeDtypeStruct((1, hid), F32),
        ),
        in_specs=[in_vmem] * 3,
        out_specs=(hbm,) * 4,
        scratch_shapes=[vmem(w_self.shape, F32), vmem(w_neigh.shape, F32), vmem((1, hid), F32), dma((4,))],
    )(hidden, s4, n4)
    return hidden, grad_self, grad_neigh, grad_bias.reshape(hid)


def solution(mesh):
    placed = (
        P("dp", "feat"),
        P("dp"),
        P("dp", None, None),
        P("dp"),
        P("dp"),
        P("dp"),
        P("dp"),
        P("feat", None),
        P("feat", None),
        P("feat"),
        P("dp", "feat"),
    )
    return jax.shard_map(
        on_device,
        mesh=mesh,
        in_specs=placed,
        out_specs=(P("dp", "feat"), P("feat", None), P("feat", None), P("feat")),
        check_vma=False,
    )
```

```python
import jax
import jax.numpy as jnp
from jax import lax
from jax.experimental import pallas as pl
from jax.experimental.pallas import tpu as pltpu
from jax.sharding import PartitionSpec as P

MESH = pl.DeviceIdType.MESH
F32 = jnp.float32
BF16 = jnp.bfloat16
NY, NZ, NX, NF = 8, 8, 4, 8
NDP = NY * NZ
BLK = 128
LANES = 128
VMEM_LIMIT = 60 * 1024 * 1024
TILE = 16


RING = (4, 5, 3, 6, 2, 7, 1)
CHIPS = (2, 1, 3)
CHUNK_ROWS = ((0, 64, False), (112, 160, True), (64, 112, False), (160, 208, True))
CHUNKS = len(CHUNK_ROWS)


def dot(a, b):
    return jnp.dot(a, b, preferred_element_type=F32)


def dot_t(a, b):
    return lax.dot_general(a, b, (((1,), (1,)), ((), ())), preferred_element_type=F32)


def kernel(
    table_hbm, ids_hbm, tiles_hbm, rows_hbm, cols_hbm, count_hbm, seed_hbm, ws_hbm, wn_hbm, bias_hbm, cot_hbm,
    hidden_hbm, s_hbm, n_hbm,
    table_f, table_b, tiles_i, tiles_f, ws_f, wn_f, w_b, w_p, cot_v, bias_v, rows_s, cols_s, count_s, seed_s,
    ids_y, ids_buf, rows_send, rows_buf, adj, x_b, x_p, xt_b,
    q_own, p_send, p_recv, sl_all, hid_v,
    *rest,
):
    pieces, rest = rest[:5 * CHUNKS], rest[5 * CHUNKS:]
    (
        loc_sem, ids_ss, idy_rs, idz_rs, rows_ss, rows_rs, q_ss, q_rs, send_sem, p_rs, sl_rs, first_rs, second_rs, third_rs,
        out_sem,
    ) = rest
    me = lax.axis_index("dp")
    feat = lax.axis_index("feat")
    y = me // NZ
    z = me % NZ
    x = feat // 2
    core = feat % 2
    fcols = table_f.shape[0]
    mate = x * 2 + 1 - core
    targets = cot_v.shape[0]

    def dp_of(yy, zz):
        return yy * NZ + zz

    own_ids = pltpu.make_async_copy(ids_hbm.at[y], ids_y.at[y], loc_sem.at[0])
    get_table = pltpu.make_async_copy(table_hbm, table_f, loc_sem.at[1])
    get_ws = pltpu.make_async_copy(ws_hbm, ws_f, loc_sem.at[2])
    get_wn = pltpu.make_async_copy(wn_hbm, wn_f, loc_sem.at[3])
    get_tiles = pltpu.make_async_copy(tiles_hbm, tiles_i, loc_sem.at[4])
    get_cot = pltpu.make_async_copy(cot_hbm, cot_v, loc_sem.at[5])
    small = [
        pltpu.make_async_copy(src, dst, loc_sem.at[6 + n])
        for n, (src, dst) in enumerate((
            (rows_hbm, rows_s), (cols_hbm, cols_s), (count_hbm, count_s), (seed_hbm, seed_s), (bias_hbm, bias_v),
        ))
    ]
    own_ids.start()

    barrier = pltpu.get_barrier_semaphore()

    for k in RING:
        pl.semaphore_signal(barrier, inc=1, device_id=(dp_of((y + k) % NY, z), feat), device_id_type=MESH)
    for k in RING:
        pl.semaphore_signal(barrier, inc=1, device_id=(dp_of(y, (z + k) % NZ), feat), device_id_type=MESH)
    for k in CHIPS:
        pl.semaphore_signal(barrier, inc=1, device_id=(me, (x + k) % NX * 2 + core), device_id_type=MESH)
    pl.semaphore_signal(barrier, inc=1, device_id=(me, mate), device_id_type=MESH)
    pl.semaphore_wait(barrier, NZ - 1 + NY - 1 + NX)

    for k in RING:
        yy = (y + k) % NY
        pltpu.make_async_remote_copy(
            ids_hbm.at[yy], ids_y.at[y], ids_ss.at[0], idy_rs,
            device_id=(dp_of(yy, z), feat), device_id_type=MESH,
        ).start()
    get_table.start()
    get_ws.start()
    get_wn.start()
    get_tiles.start()
    for copy in small:
        copy.start()
    get_cot.start()
    own_ids.wait()
    pltpu.make_async_copy(ids_y.at[pl.ds(0, NY - 1)], ids_y.at[pl.ds(0, NY - 1)], idy_rs).wait()
    for k in RING:
        pltpu.make_async_remote_copy(
            ids_y, ids_buf.at[z], ids_ss.at[1], idz_rs,
            device_id=(dp_of(y, (z + k) % NZ), feat), device_id_type=MESH,
        ).start()
    ids_buf[z] = ids_y[...]

    get_table.wait()
    table_b[...] = table_f[...].astype(BF16)
    pltpu.make_async_copy(ids_buf.at[pl.ds(0, NZ - 1)], ids_buf.at[pl.ds(0, NZ - 1)], idz_rs).wait()

    lane = lax.broadcasted_iota(jnp.int32, (NZ, TILE, LANES), 2)
    slot = lax.broadcasted_iota(jnp.int32, (NZ, TILE, LANES), 1)
    mine = lane == z * TILE + slot
    table_rows = table_b.shape[1]
    row_of = lax.broadcasted_iota(jnp.int32, (NZ * TILE, table_rows), 1)

    def gather(step, c):
        pair = ((y + 4 - step) % NY, (y + 5 + step) % NY)
        for yy in pair:
            asked = ids_buf[:, yy].astype(F32)
            picked = jnp.where(mine, jnp.broadcast_to(asked, (NZ, TILE, LANES)), 0.0)
            column = jnp.sum(picked.reshape(NZ * TILE, LANES), axis=1, keepdims=True).astype(jnp.int32)
            hot = jnp.where(column == row_of, 1.0, 0.0).astype(BF16)
            found = dot_t(hot, table_b[...]).astype(BF16)
            rows_send[pl.ds(yy * NZ, NZ)] = found.reshape(NZ, TILE, fcols)
        for dz in RING + (0,):
            zz = (z + dz) % NZ
            for yy in pair:
                to = dp_of(yy, zz)
                copy = pltpu.make_async_remote_copy(
                    rows_send.at[to], rows_buf.at[me], rows_ss, rows_rs,
                    device_id=(to, feat), device_id_type=MESH,
                )
                if dz == 0:
                    pl.when(to != me)(copy.start)
                else:
                    copy.start()
        return c

    lax.fori_loop(0, NY // 2, gather, 0)
    rows_buf[me] = rows_send[me]

    get_ws.wait()
    get_wn.wait()
    w_b[...] = jnp.zeros_like(w_b)
    x_b[...] = jnp.zeros_like(x_b)
    for c in range(NX):
        for co in range(2):
            at = (c * 2 + co) * LANES
            w_b[co, c, :fcols] = ws_f[:, at:at + LANES].astype(BF16)
            w_b[co, c, LANES:LANES + fcols] = wn_f[:, at:at + LANES].astype(BF16)
    w_copy = pltpu.make_async_remote_copy(
        w_b.at[1 - core], w_p, q_ss.at[0], q_rs.at[0], device_id=(me, mate), device_id_type=MESH
    )
    w_copy.start()
    get_tiles.wait()
    tiles_f[...] = tiles_i[...].astype(F32)
    n_slots = tiles_f.shape[0]
    for copy in small:
        copy.wait()
    col_blocks = adj.shape[1] // BLK

    def place(i, c):
        r = i // col_blocks
        q = i % col_blocks
        total = jnp.zeros((BLK, BLK), F32)
        for k in range(n_slots):
            on = (rows_s[k] == r) & (cols_s[k] == q) & (k < count_s[0])
            total = total + tiles_f[k] * jnp.where(on, 1.0, 0.0)
        adj[pl.ds(pl.multiple_of(r * BLK, BLK), BLK), pl.ds(pl.multiple_of(q * BLK, BLK), BLK)] = total.astype(BF16)
        return c

    lax.fori_loop(0, (targets // BLK) * col_blocks, place, 0)
    degree = jnp.sum(adj[...].astype(F32), axis=1, keepdims=True)
    scale = 1.0 / jnp.maximum(degree, 1.0)
    get_cot.wait()
    w_copy.wait_recv()

    pltpu.make_async_copy(rows_buf.at[pl.ds(0, NDP - 1)], rows_buf.at[pl.ds(0, NDP - 1)], rows_rs).wait()
    sampled = rows_buf[...].reshape(NDP * TILE, fcols)
    self_rows = sampled[:targets]
    neigh = dot(adj[...], sampled) * scale
    x_b[0, :, :fcols] = self_rows
    x_b[1, :, :fcols] = neigh.astype(BF16)
    x_copy = pltpu.make_async_remote_copy(
        x_b, x_p, q_ss.at[1], q_rs.at[1], device_id=(me, mate), device_id_type=MESH
    )
    x_copy.start()

    both = jnp.concatenate([x_b[0], x_b[1]], axis=1)
    for k in CHIPS + (0,):
        chip = (x + k) % NX
        q_own[chip] = dot(both, w_b[core, chip])
    x_copy.wait_recv()
    other = jnp.concatenate([x_p[0], x_p[1]], axis=1)
    for k in CHIPS:
        chip = (x + k) % NX
        p_send[chip] = (q_own[chip] + dot(other, w_p[chip])).astype(BF16)
        pltpu.make_async_remote_copy(
            p_send.at[chip], p_recv.at[x], send_sem.at[3 * CHUNKS], p_rs.at[x],
            device_id=(me, chip * 2 + core), device_id_type=MESH,
        ).start()
    preact = q_own[x] + dot(other, w_p[x]) + bias_v[...]

    xs_t = self_rows.astype(F32).T
    xn_t = neigh.T
    ones = jnp.where(lax.broadcasted_iota(jnp.int32, (TILE, targets), 0) == 0, 1.0, 0.0)
    xt_b[:fcols] = xs_t.astype(BF16)
    xt_b[fcols:fcols + TILE] = ones.astype(BF16)
    xt_b[fcols + TILE:] = xn_t.astype(BF16)

    for k in (1, 3, 2):
        frm = (x + k) % NX
        pltpu.make_async_copy(p_recv.at[frm], p_recv.at[frm], p_rs.at[frm]).wait()
        preact = preact + p_recv[frm].astype(F32)
    alive = jnp.where(lax.broadcasted_iota(jnp.int32, (targets, LANES), 0) < seed_s[0], 1.0, 0.0)
    sigma = jax.nn.sigmoid(preact)
    slope = cot_v[...].astype(F32) * alive * sigma * (1.0 + preact * (1.0 - sigma))
    sl_all[feat] = slope.astype(BF16)

    def slope_copy(which, sem, to):
        return pltpu.make_async_remote_copy(
            sl_all.at[which], sl_all.at[which], sem, sl_rs.at[which],
            device_id=(me, to), device_id_type=MESH,
        )

    for k in CHIPS:
        slope_copy(feat, send_sem.at[3 * CHUNKS + 1], (x + k) % NX * 2 + core).start()
    slope_copy(feat, q_ss.at[2], mate).start()
    hid_v[...] = (preact * sigma * alive).astype(BF16)
    put_hidden = pltpu.make_async_copy(hid_v, hidden_hbm, out_sem.at[0])
    put_hidden.start()

    def line(across, k):
        if across:
            return dp_of((y + k) % NY, z)
        return dp_of(y, (z + k) % NZ)

    class Chunk:
        def __init__(self, n):
            self.low, self.high, self.across = CHUNK_ROWS[n]
            self.send, self.recv, self.own, self.second, self.total = pieces[5 * n:5 * n + 5]
            self.here, self.there = (y, z) if self.across else (z, y)
            self.n = n
            base = 0 if self.low < s_rows else s_rows
            self.out = (n_hbm if self.across else s_hbm).at[:, pl.ds(self.low - base, self.high - self.low)]

        def first(self, at, grad):
            part = grad[self.low:self.high]

            @pl.when(at == self.here)
            def _():
                self.own[...] = part

            @pl.when(at != self.here)
            def _():
                self.send[at] = part.astype(BF16)
                to = dp_of(at, z) if self.across else dp_of(y, at)
                pltpu.make_async_remote_copy(
                    self.send.at[at], self.recv.at[self.here], send_sem.at[self.n], first_rs.at[self.n, self.here],
                    device_id=(to, feat), device_id_type=MESH,
                ).start()

        def add_first(self):
            total = self.own[...]
            for k in RING:
                frm = (self.here - k + NZ) % NZ
                pltpu.make_async_copy(self.recv.at[frm], self.recv.at[frm], first_rs.at[self.n, frm]).wait()
                total = total + self.recv[frm].astype(F32)
            self.second[self.there] = total.astype(BF16)
            for k in RING:
                pltpu.make_async_remote_copy(
                    self.second.at[self.there], self.second.at[self.there],
                    send_sem.at[CHUNKS + self.n], second_rs.at[self.n, self.there],
                    device_id=(line(not self.across, k), feat), device_id_type=MESH,
                ).start()

        def add_second(self):
            for k in RING:
                frm = (self.there - k + NZ) % NZ
                pltpu.make_async_copy(self.second.at[frm], self.second.at[frm], second_rs.at[self.n, frm]).wait()
            total = self.second[0].astype(F32)
            for n in range(1, NZ):
                total = total + self.second[n].astype(F32)
            self.total[...] = total.astype(BF16)
            for k in RING:
                pltpu.make_async_remote_copy(
                    self.total, self.out.at[self.here], send_sem.at[2 * CHUNKS + self.n], third_rs.at[self.n, self.here],
                    device_id=(line(self.across, k), feat), device_id_type=MESH,
                ).start()
            self.keep().start()

        def keep(self):
            return pltpu.make_async_copy(self.total, self.out.at[self.here], out_sem.at[1 + self.n])

        def finish(self):
            for k in RING:
                frm = (self.here - k + NZ) % NZ
                pltpu.make_async_copy(self.out.at[frm], self.out.at[frm], third_rs.at[self.n, frm]).wait()
            self.keep().wait()

    s_rows = fcols + TILE
    chunks = [Chunk(n) for n in range(CHUNKS)]

    def first(block):
        grad = dot(xt_b[...], sl_all[block])
        for chunk in chunks:
            chunk.first(block // 2 + block % 2 * NX, grad)

    def wait_slope(which):
        pltpu.make_async_copy(sl_all.at[which], sl_all.at[which], sl_rs.at[which]).wait()

    first(feat)
    wait_slope(mate)
    first(mate)
    for n, k in enumerate((1, 3, 2)):
        direct = (x + k) % NX * 2 + core
        passed = (x + k) % NX * 2 + 1 - core
        wait_slope(direct)
        slope_copy(direct, q_ss.at[3 + n], mate).start()
        first(direct)
        wait_slope(passed)
        first(passed)

    for chunk in chunks:
        chunk.add_first()
    for chunk in chunks:
        chunk.add_second()
    for chunk in chunks:
        chunk.finish()
    put_hidden.wait()

    def sent(buf, count, sem):
        pltpu.make_async_copy(buf.at[pl.ds(0, count)], buf.at[pl.ds(0, count)], sem).wait()

    sent(ids_y, NY - 1, ids_ss.at[0])
    sent(ids_buf, NZ - 1, ids_ss.at[1])
    sent(rows_send, NDP - 1, rows_ss)
    sent(p_send, NX - 1, send_sem.at[3 * CHUNKS])
    sent(sl_all, NX - 1, send_sem.at[3 * CHUNKS + 1])
    for chunk in chunks:
        sent(chunk.send, NZ - 1, send_sem.at[chunk.n])
        sent(chunk.second, NZ - 1, send_sem.at[CHUNKS + chunk.n])
        sent(chunk.send, NZ - 1, send_sem.at[2 * CHUNKS + chunk.n])
    w_copy.wait_send()
    x_copy.wait_send()
    for c in range(NX):
        sent(sl_all, 1, q_ss.at[2 + c])


def finish(hidden_in, s_in, n_in, hidden_ref, gself_ref, gneigh_ref, gbias_ref, gs_v, gn_v, gb_v, sem):
    fcols = gs_v.shape[0]
    copies = [pltpu.make_async_copy(hidden_in, hidden_ref, sem.at[0])]
    copies[0].start()
    for t in range(NF):
        c = (t % NX) * 2 + t // NX
        gs_v[:, c * LANES:(c + 1) * LANES] = s_in[t][:fcols].astype(F32)
    copies.append(pltpu.make_async_copy(gs_v, gself_ref, sem.at[1]))
    copies[1].start()
    for t in range(NF):
        c = (t % NX) * 2 + t // NX
        gn_v[:, c * LANES:(c + 1) * LANES] = n_in[t].astype(F32)
    copies.append(pltpu.make_async_copy(gn_v, gneigh_ref, sem.at[2]))
    copies[2].start()
    feat = lax.axis_index("feat")
    gb_v[...] = s_in[feat // 2 + feat % 2 * NX][fcols:fcols + TILE].astype(F32)[:1]
    copies.append(pltpu.make_async_copy(gb_v, gbias_ref, sem.at[3]))
    copies[3].start()
    for copy in copies:
        copy.wait()


def on_device(table, node_ids, tiles, tile_rows, tile_cols, tile_count, seed_count, w_self, w_neigh, bias, cotangent):
    fcols = table.shape[1]
    hidden_all = w_self.shape[1]
    targets, hid = cotangent.shape
    s_rows, n_rows = fcols + TILE, fcols
    vmem = pltpu.VMEM
    dma = pltpu.SemaphoreType.DMA
    hbm = pl.BlockSpec(memory_space=pl.ANY)
    scratch = [
        vmem(table.shape[::-1], F32),
        vmem(table.shape[::-1], BF16),
        vmem(tiles.shape, jnp.int32),
        vmem(tiles.shape, F32),
        vmem(w_self.shape, F32),
        vmem(w_neigh.shape, F32),
        vmem((2, NX, 2 * LANES, LANES), BF16),
        vmem((NX, 2 * LANES, LANES), BF16),
        vmem(cotangent.shape, BF16),
        vmem((1, hid), F32),
        pltpu.SMEM(tile_rows.shape, jnp.int32),
        pltpu.SMEM(tile_cols.shape, jnp.int32),
        pltpu.SMEM(tile_count.shape, jnp.int32),
        pltpu.SMEM(seed_count.shape, jnp.int32),
        vmem((NY, 1, LANES), jnp.int32),
        vmem((NZ, NY, 1, LANES), jnp.int32),
        vmem((NDP, TILE, fcols), BF16),
        vmem((NDP, TILE, fcols), BF16),
        vmem((targets, NDP * TILE), BF16),
        vmem((2, targets, LANES), BF16),
        vmem((2, targets, LANES), BF16),
        vmem((s_rows + n_rows, targets), BF16),
        vmem((NX, targets, hid), F32),
        vmem((NX, targets, hid), BF16),
        vmem((NX, targets, hid), BF16),
        vmem((NF, targets, hid), BF16),
        vmem((targets, hid), BF16),
    ]
    for low, high, _ in CHUNK_ROWS:
        rows = high - low
        scratch += [
            vmem((NZ, rows, LANES), BF16),
            vmem((NZ, rows, LANES), BF16),
            vmem((rows, LANES), F32),
            vmem((NZ, rows, LANES), BF16),
            vmem((rows, LANES), BF16),
        ]
    scratch += [
        dma((11,)),
        dma((2,)), dma, dma, dma, dma,
        dma((2 + NX,)), dma((2,)),
        dma((3 * CHUNKS + 2,)),
        dma((NX,)), dma((NF,)),
        dma((CHUNKS, NZ)), dma((CHUNKS, NZ)), dma((CHUNKS, NZ)),
        dma((1 + CHUNKS,)),
    ]
    hidden, s4, n4 = pl.pallas_call(
        kernel,
        out_shape=(
            jax.ShapeDtypeStruct((targets, hid), BF16),
            jax.ShapeDtypeStruct((NZ, s_rows, LANES), BF16),
            jax.ShapeDtypeStruct((NY, n_rows, LANES), BF16),
        ),
        in_specs=[hbm] * 11,
        out_specs=(hbm,) * 3,
        scratch_shapes=scratch,
        compiler_params=pltpu.CompilerParams(
            collective_id=0, has_side_effects=True, vmem_limit_bytes=VMEM_LIMIT
        ),
        cost_estimate=pl.CostEstimate(flops=300_000_000, bytes_accessed=4_000_000, transcendentals=65536),
    )(
        table.T, node_ids.reshape(NY, 1, NZ * TILE), tiles, tile_rows, tile_cols,
        tile_count, seed_count, w_self, w_neigh, bias.reshape(1, hid), cotangent,
    )
    hidden, grad_self, grad_neigh, grad_bias = pl.pallas_call(
        finish,
        out_shape=(
            jax.ShapeDtypeStruct((targets, hid), BF16),
            jax.ShapeDtypeStruct(w_self.shape, F32),
            jax.ShapeDtypeStruct(w_neigh.shape, F32),
            jax.ShapeDtypeStruct((1, hid), F32),
        ),
        in_specs=[pl.BlockSpec(memory_space=pltpu.VMEM)] * 3,
        out_specs=(hbm,) * 4,
        scratch_shapes=[
            vmem(w_self.shape, F32), vmem(w_neigh.shape, F32), vmem((1, hid), F32), dma((4,)),
        ],
    )(hidden, s4, n4)
    return hidden, grad_self, grad_neigh, grad_bias.reshape(hid)


def solution(mesh):
    placed = (
        P("dp", "feat"),
        P("dp"),
        P("dp", None, None),
        P("dp"),
        P("dp"),
        P("dp"),
        P("dp"),
        P("feat", None),
        P("feat", None),
        P("feat"),
        P("dp", "feat"),
    )
    return jax.shard_map(
        on_device,
        mesh=mesh,
        in_specs=placed,
        out_specs=(P("dp", "feat"), P("feat", None), P("feat", None), P("feat")),
        check_vma=False,
    )
```

```python
import jax
import jax.numpy as jnp
from jax import lax
from jax.experimental import pallas as pl
from jax.experimental.pallas import tpu as pltpu
from jax.sharding import PartitionSpec as P

MESH = pl.DeviceIdType.MESH
F32 = jnp.float32
BF16 = jnp.bfloat16
NY, NZ, NX, NF = 8, 8, 4, 8
NDP = NY * NZ
BLK = 128
LANES = 128
VMEM_LIMIT = 60 * 1024 * 1024
TILE = 16


RING = (4, 5, 3, 6, 2, 7, 1)


def hops(offset):
    return min(offset[0], NY - offset[0]) + min(offset[1], NZ - offset[1])


FARTHEST = sorted(((a, b) for a in range(NY) for b in range(NZ) if a or b), key=lambda o: (-hops(o), o))
CHIPS = (2, 1, 3)
CHUNK_ROWS = ((0, 64, False), (112, 160, True), (64, 112, False), (160, 208, True))
CHUNKS = len(CHUNK_ROWS)
HALVES = 2


def dot(a, b):
    return jnp.dot(a, b, preferred_element_type=F32)


def dot_t(a, b):
    return lax.dot_general(a, b, (((1,), (1,)), ((), ())), preferred_element_type=F32)


def kernel(
    table_hbm, ids_hbm, tiles_hbm, rows_hbm, cols_hbm, count_hbm, seed_hbm, ws_hbm, wn_hbm, bias_hbm, cot_hbm,
    hidden_hbm, s_hbm, n_hbm,
    table_f, table_b, tiles_i, tiles_f, ws_f, wn_f, w_b, w_p, cot_v, bias_v, rows_s, cols_s, count_s, seed_s,
    ids_v, ids_y, ids_buf, rows_send, rows_buf, adj, x_b, x_p, xt_b,
    q_own, p_send, p_recv, sl_all, hid_v,
    *rest,
):
    pieces, rest = rest[:5 * CHUNKS], rest[5 * CHUNKS:]
    (
        loc_sem, ids_ss, idy_rs, idz_rs, rows_ss, rows_rs, q_ss, q_rs, f_ss, send_sem, p_rs, sl_rs, first_rs, second_rs, third_rs,
        out_sem,
    ) = rest
    me = lax.axis_index("dp")
    feat = lax.axis_index("feat")
    y = me // NZ
    z = me % NZ
    x = feat // 2
    core = feat % 2
    fcols = table_f.shape[0]
    mate = x * 2 + 1 - core
    targets = cot_v.shape[0]

    def dp_of(yy, zz):
        return yy * NZ + zz

    own_ids = pltpu.make_async_copy(ids_hbm, ids_v, loc_sem.at[0])
    get_table = pltpu.make_async_copy(table_hbm, table_f, loc_sem.at[1])
    get_ws = pltpu.make_async_copy(ws_hbm, ws_f, loc_sem.at[2])
    get_wn = pltpu.make_async_copy(wn_hbm, wn_f, loc_sem.at[3])
    get_tiles = pltpu.make_async_copy(tiles_hbm, tiles_i, loc_sem.at[4])
    get_cot = pltpu.make_async_copy(cot_hbm, cot_v, loc_sem.at[5])
    small = [
        pltpu.make_async_copy(src, dst, loc_sem.at[6 + n])
        for n, (src, dst) in enumerate((
            (rows_hbm, rows_s), (cols_hbm, cols_s), (count_hbm, count_s), (seed_hbm, seed_s), (bias_hbm, bias_v),
        ))
    ]
    own_ids.start()

    barrier = pltpu.get_barrier_semaphore()

    for k in RING:
        pl.semaphore_signal(barrier, inc=1, device_id=(dp_of((y + k) % NY, z), feat), device_id_type=MESH)
    for k in RING:
        pl.semaphore_signal(barrier, inc=1, device_id=(dp_of(y, (z + k) % NZ), feat), device_id_type=MESH)
    for k in CHIPS:
        pl.semaphore_signal(barrier, inc=1, device_id=(me, (x + k) % NX * 2 + core), device_id_type=MESH)
    pl.semaphore_signal(barrier, inc=1, device_id=(me, mate), device_id_type=MESH)
    pl.semaphore_wait(barrier, NZ - 1 + NY - 1 + NX)

    own_ids.wait()
    for k in RING:
        yy = (y + k) % NY
        pltpu.make_async_remote_copy(
            ids_v.at[yy], ids_y.at[y], ids_ss.at[0], idy_rs,
            device_id=(dp_of(yy, z), feat), device_id_type=MESH,
        ).start()
    get_table.start()
    get_ws.start()
    get_wn.start()
    get_tiles.start()
    for copy in small:
        copy.start()
    get_cot.start()
    ids_y[y] = ids_v[y]
    pltpu.make_async_copy(ids_y.at[pl.ds(0, NY - 1)], ids_y.at[pl.ds(0, NY - 1)], idy_rs).wait()
    for k in RING:
        pltpu.make_async_remote_copy(
            ids_y, ids_buf.at[z], ids_ss.at[1], idz_rs,
            device_id=(dp_of(y, (z + k) % NZ), feat), device_id_type=MESH,
        ).start()
    ids_buf[z] = ids_y[...]

    get_table.wait()
    table_b[...] = table_f[...].astype(BF16)
    pltpu.make_async_copy(ids_buf.at[pl.ds(0, NZ - 1)], ids_buf.at[pl.ds(0, NZ - 1)], idz_rs).wait()

    lane = lax.broadcasted_iota(jnp.int32, (NZ, TILE, LANES), 2)
    slot = lax.broadcasted_iota(jnp.int32, (NZ, TILE, LANES), 1)
    mine = lane == z * TILE + slot
    table_rows = table_b.shape[1]
    row_of = lax.broadcasted_iota(jnp.int32, (NZ * TILE, table_rows), 1)

    def gather(step, c):
        pair = ((y + 4 - step) % NY, (y + 5 + step) % NY)
        for yy in pair:
            asked = ids_buf[:, yy].astype(F32)
            picked = jnp.where(mine, jnp.broadcast_to(asked, (NZ, TILE, LANES)), 0.0)
            column = jnp.sum(picked.reshape(NZ * TILE, LANES), axis=1, keepdims=True).astype(jnp.int32)
            hot = jnp.where(column == row_of, 1.0, 0.0).astype(BF16)
            found = dot_t(hot, table_b[...]).astype(BF16)
            rows_send[pl.ds(yy * NZ, NZ)] = found.reshape(NZ, TILE, fcols)
        return c

    def send_rows(chosen):
        for dy, dz in chosen:
            to = dp_of((y + dy) % NY, (z + dz) % NZ)
            pltpu.make_async_remote_copy(
                rows_send.at[to], rows_buf.at[me], rows_ss, rows_rs,
                device_id=(to, feat), device_id_type=MESH,
            ).start()

    lax.fori_loop(0, 2, gather, 0)
    early = [o for o in FARTHEST if o[0] in (3, 4, 5, 6) and hops(o) > 5]
    send_rows(early)
    lax.fori_loop(2, NY // 2, gather, 0)
    send_rows([o for o in FARTHEST if o not in early])
    rows_buf[me] = rows_send[me]

    get_ws.wait()
    get_wn.wait()
    w_b[...] = jnp.zeros_like(w_b)
    x_b[...] = jnp.zeros_like(x_b)
    for c in range(NX):
        for co in range(2):
            at = (c * 2 + co) * LANES
            w_b[co, c, :fcols] = ws_f[:, at:at + LANES].astype(BF16)
            w_b[co, c, LANES:LANES + fcols] = wn_f[:, at:at + LANES].astype(BF16)
    w_copy = pltpu.make_async_remote_copy(
        w_b.at[1 - core], w_p, q_ss.at[0], q_rs.at[0], device_id=(me, mate), device_id_type=MESH
    )
    w_copy.start()
    get_tiles.wait()
    tiles_f[...] = tiles_i[...].astype(F32)
    n_slots = tiles_f.shape[0]
    for copy in small:
        copy.wait()
    col_blocks = adj.shape[1] // BLK

    def place(i, c):
        r = i // col_blocks
        q = i % col_blocks
        total = jnp.zeros((BLK, BLK), F32)
        for k in range(n_slots):
            on = (rows_s[k] == r) & (cols_s[k] == q) & (k < count_s[0])
            total = total + tiles_f[k] * jnp.where(on, 1.0, 0.0)
        adj[pl.ds(pl.multiple_of(r * BLK, BLK), BLK), pl.ds(pl.multiple_of(q * BLK, BLK), BLK)] = total.astype(BF16)
        return c

    lax.fori_loop(0, (targets // BLK) * col_blocks, place, 0)
    degree = jnp.sum(adj[...].astype(F32), axis=1, keepdims=True)
    scale = 1.0 / jnp.maximum(degree, 1.0)
    get_cot.wait()
    w_copy.wait_recv()

    pltpu.make_async_copy(rows_buf.at[pl.ds(0, NDP - 1)], rows_buf.at[pl.ds(0, NDP - 1)], rows_rs).wait()
    sampled = rows_buf[...].reshape(NDP * TILE, fcols)
    self_rows = sampled[:targets]
    neigh = dot(adj[...], sampled) * scale
    x_b[0, :, :fcols] = self_rows
    x_b[1, :, :fcols] = neigh.astype(BF16)
    x_copy = pltpu.make_async_remote_copy(
        x_b, x_p, q_ss.at[1], q_rs.at[1], device_id=(me, mate), device_id_type=MESH
    )
    x_copy.start()

    both = jnp.concatenate([x_b[0], x_b[1]], axis=1)
    for k in CHIPS + (0,):
        chip = (x + k) % NX
        q_own[chip] = dot(both, w_b[core, chip])
    x_copy.wait_recv()
    other = jnp.concatenate([x_p[0], x_p[1]], axis=1)
    half = targets // HALVES
    for h in range(HALVES):
        low = h * half
        for k in CHIPS:
            chip = (x + k) % NX
            own = q_own[chip, low:low + half]
            p_send[h, chip] = (own + dot(other[low:low + half], w_p[chip])).astype(BF16)
            pltpu.make_async_remote_copy(
                p_send.at[h, chip], p_recv.at[h, x], send_sem.at[3 * CHUNKS + h], p_rs.at[h, x],
                device_id=(me, chip * 2 + core), device_id_type=MESH,
            ).start()
    preact = q_own[x] + dot(other, w_p[x]) + bias_v[...]

    xs_t = self_rows.astype(F32).T
    xn_t = neigh.T
    ones = jnp.where(lax.broadcasted_iota(jnp.int32, (TILE, targets), 0) == 0, 1.0, 0.0)
    xt_b[:fcols] = xs_t.astype(BF16)
    xt_b[fcols:fcols + TILE] = ones.astype(BF16)
    xt_b[fcols + TILE:] = xn_t.astype(BF16)

    def slope_copy(which, h, sem, to):
        return pltpu.make_async_remote_copy(
            sl_all.at[which, h], sl_all.at[which, h], sem, sl_rs.at[which, h],
            device_id=(me, to), device_id_type=MESH,
        )

    def activate(h):
        low = h * half
        total = preact[low:low + half]
        for k in (1, 3, 2):
            frm = (x + k) % NX
            pltpu.make_async_copy(p_recv.at[h, frm], p_recv.at[h, frm], p_rs.at[h, frm]).wait()
            total = total + p_recv[h, frm].astype(F32)
        row = low + lax.broadcasted_iota(jnp.int32, (half, LANES), 0)
        alive = jnp.where(row < seed_s[0], 1.0, 0.0)
        sigma = jax.nn.sigmoid(total)
        slope = cot_v[low:low + half].astype(F32) * alive * sigma * (1.0 + total * (1.0 - sigma))
        sl_all[feat, h] = slope.astype(BF16)
        for k in CHIPS:
            slope_copy(feat, h, send_sem.at[3 * CHUNKS + HALVES + h], (x + k) % NX * 2 + core).start()
        slope_copy(feat, h, f_ss.at[0, h], mate).start()
        hid_v[low:low + half] = (total * sigma * alive).astype(BF16)

    for h in range(HALVES):
        activate(h)
    put_hidden = pltpu.make_async_copy(hid_v, hidden_hbm, out_sem.at[0])
    put_hidden.start()

    def line(across, k):
        if across:
            return dp_of((y + k) % NY, z)
        return dp_of(y, (z + k) % NZ)

    class Chunk:
        def __init__(self, n):
            self.low, self.high, self.across = CHUNK_ROWS[n]
            self.send, self.recv, self.own, self.second, self.total = pieces[5 * n:5 * n + 5]
            self.here, self.there = (y, z) if self.across else (z, y)
            self.n = n
            base = 0 if self.low < s_rows else s_rows
            self.out = (n_hbm if self.across else s_hbm).at[:, pl.ds(self.low - base, self.high - self.low)]

        def first(self, at, grad):
            part = grad[self.low:self.high]

            @pl.when(at == self.here)
            def _():
                self.own[...] = part

            @pl.when(at != self.here)
            def _():
                self.send[at] = part.astype(BF16)
                to = dp_of(at, z) if self.across else dp_of(y, at)
                pltpu.make_async_remote_copy(
                    self.send.at[at], self.recv.at[self.here], send_sem.at[self.n], first_rs.at[self.n, self.here],
                    device_id=(to, feat), device_id_type=MESH,
                ).start()

        def add_first(self):
            total = self.own[...]
            for k in RING:
                frm = (self.here - k + NZ) % NZ
                pltpu.make_async_copy(self.recv.at[frm], self.recv.at[frm], first_rs.at[self.n, frm]).wait()
                total = total + self.recv[frm].astype(F32)
            self.second[self.there] = total.astype(BF16)
            for k in RING:
                pltpu.make_async_remote_copy(
                    self.second.at[self.there], self.second.at[self.there],
                    send_sem.at[CHUNKS + self.n], second_rs.at[self.n, self.there],
                    device_id=(line(not self.across, k), feat), device_id_type=MESH,
                ).start()

        def add_second(self):
            for k in RING:
                frm = (self.there - k + NZ) % NZ
                pltpu.make_async_copy(self.second.at[frm], self.second.at[frm], second_rs.at[self.n, frm]).wait()
            total = self.second[0].astype(F32)
            for n in range(1, NZ):
                total = total + self.second[n].astype(F32)
            self.total[...] = total.astype(BF16)
            for k in RING:
                pltpu.make_async_remote_copy(
                    self.total, self.out.at[self.here], send_sem.at[2 * CHUNKS + self.n], third_rs.at[self.n, self.here],
                    device_id=(line(self.across, k), feat), device_id_type=MESH,
                ).start()
            self.keep().start()

        def keep(self):
            return pltpu.make_async_copy(self.total, self.out.at[self.here], out_sem.at[1 + self.n])

        def finish(self):
            for k in RING:
                frm = (self.here - k + NZ) % NZ
                pltpu.make_async_copy(self.out.at[frm], self.out.at[frm], third_rs.at[self.n, frm]).wait()
            self.keep().wait()

    s_rows = fcols + TILE
    chunks = [Chunk(n) for n in range(CHUNKS)]

    def first(block):
        grad = dot(xt_b[...], sl_all[block].reshape(targets, LANES))
        for chunk in chunks:
            chunk.first(block // 2 + block % 2 * NX, grad)

    def wait_slope(which, h):
        pltpu.make_async_copy(sl_all.at[which, h], sl_all.at[which, h], sl_rs.at[which, h]).wait()

    first(feat)
    for h in range(HALVES):
        wait_slope(mate, h)
    first(mate)
    for n, k in enumerate((1, 3, 2)):
        direct = (x + k) % NX * 2 + core
        passed = (x + k) % NX * 2 + 1 - core
        for h in range(HALVES):
            wait_slope(direct, h)
            slope_copy(direct, h, f_ss.at[1 + n, h], mate).start()
        first(direct)
        for h in range(HALVES):
            wait_slope(passed, h)
        first(passed)

    for chunk in chunks:
        chunk.add_first()
    for chunk in chunks:
        chunk.add_second()
    for chunk in chunks:
        chunk.finish()
    put_hidden.wait()

    def sent(buf, count, sem):
        pltpu.make_async_copy(buf.at[pl.ds(0, count)], buf.at[pl.ds(0, count)], sem).wait()

    sent(ids_y, NY - 1, ids_ss.at[0])
    sent(ids_buf, NZ - 1, ids_ss.at[1])
    sent(rows_send, NDP - 1, rows_ss)
    for h in range(HALVES):
        sent(p_send.at[h], NX - 1, send_sem.at[3 * CHUNKS + h])
        sent(p_send.at[h], NX - 1, send_sem.at[3 * CHUNKS + HALVES + h])
    for chunk in chunks:
        sent(chunk.send, NZ - 1, send_sem.at[chunk.n])
        sent(chunk.second, NZ - 1, send_sem.at[CHUNKS + chunk.n])
        sent(chunk.send, NZ - 1, send_sem.at[2 * CHUNKS + chunk.n])
    w_copy.wait_send()
    x_copy.wait_send()
    for c in range(NX):
        for h in range(HALVES):
            pltpu.make_async_copy(sl_all.at[c, h], sl_all.at[c, h], f_ss.at[c, h]).wait()


def finish(
    hidden_in, s_in, n_in, hidden_ref, gself_ref, gneigh_ref, gbias_ref, h_v, s_v, n_v, gs_v, gn_v, gb_v, in_sem, out_sem
):
    fcols = gs_v.shape[0]
    gets = []
    for n, (src, dst) in enumerate(((s_in, s_v), (n_in, n_v))):
        for part in range(2):
            rows = pl.ds(part * NX, NX)
            gets.append(pltpu.make_async_copy(src.at[rows], dst.at[rows], in_sem.at[n * 2 + part]))
    for copy in gets:
        copy.start()
    get_hidden = pltpu.make_async_copy(hidden_in, h_v, in_sem.at[4])
    get_hidden.start()
    puts = []

    def put(src, dst):
        puts.append(pltpu.make_async_copy(src, dst, out_sem.at[len(puts)]))
        puts[-1].start()

    feat = lax.axis_index("feat")
    for src, dst, base, out in ((s_v, gs_v, 0, gself_ref), (n_v, gn_v, 2, gneigh_ref)):
        for part in range(2):
            gets[base + part].wait()
            for t in range(part * NX, part * NX + NX):
                c = (t % NX) * 2 + t // NX
                dst[:, c * LANES:(c + 1) * LANES] = src[t][:fcols].astype(F32)
        if base == 0:
            gb_v[...] = s_v[feat // 2 + feat % 2 * NX][fcols:fcols + TILE].astype(F32)[:1]
            put(gb_v, gbias_ref)
        put(dst, out)
        if base == 0:
            get_hidden.wait()
            put(h_v, hidden_ref)
    for copy in puts:
        copy.wait()


def on_device(table, node_ids, tiles, tile_rows, tile_cols, tile_count, seed_count, w_self, w_neigh, bias, cotangent):
    fcols = table.shape[1]
    hidden_all = w_self.shape[1]
    targets, hid = cotangent.shape
    s_rows, n_rows = fcols + TILE, fcols
    vmem = pltpu.VMEM
    dma = pltpu.SemaphoreType.DMA
    hbm = pl.BlockSpec(memory_space=pl.ANY)
    scratch = [
        vmem(table.shape[::-1], F32),
        vmem(table.shape[::-1], BF16),
        vmem(tiles.shape, jnp.int32),
        vmem(tiles.shape, F32),
        vmem(w_self.shape, F32),
        vmem(w_neigh.shape, F32),
        vmem((2, NX, 2 * LANES, LANES), BF16),
        vmem((NX, 2 * LANES, LANES), BF16),
        vmem(cotangent.shape, BF16),
        vmem((1, hid), F32),
        pltpu.SMEM(tile_rows.shape, jnp.int32),
        pltpu.SMEM(tile_cols.shape, jnp.int32),
        pltpu.SMEM(tile_count.shape, jnp.int32),
        pltpu.SMEM(seed_count.shape, jnp.int32),
        vmem((NY, 1, LANES), jnp.int32),
        vmem((NY, 1, LANES), jnp.int32),
        vmem((NZ, NY, 1, LANES), jnp.int32),
        vmem((NDP, TILE, fcols), BF16),
        vmem((NDP, TILE, fcols), BF16),
        vmem((targets, NDP * TILE), BF16),
        vmem((2, targets, LANES), BF16),
        vmem((2, targets, LANES), BF16),
        vmem((s_rows + n_rows, targets), BF16),
        vmem((NX, targets, hid), F32),
        vmem((HALVES, NX, targets // HALVES, hid), BF16),
        vmem((HALVES, NX, targets // HALVES, hid), BF16),
        vmem((NF, HALVES, targets // HALVES, hid), BF16),
        vmem((targets, hid), BF16),
    ]
    for low, high, _ in CHUNK_ROWS:
        rows = high - low
        scratch += [
            vmem((NZ, rows, LANES), BF16),
            vmem((NZ, rows, LANES), BF16),
            vmem((rows, LANES), F32),
            vmem((NZ, rows, LANES), BF16),
            vmem((rows, LANES), BF16),
        ]
    scratch += [
        dma((11,)),
        dma((2,)), dma, dma, dma, dma,
        dma((2,)), dma((2,)), dma((NX, HALVES)),
        dma((3 * CHUNKS + 2 * HALVES,)),
        dma((HALVES, NX)), dma((NF, HALVES)),
        dma((CHUNKS, NZ)), dma((CHUNKS, NZ)), dma((CHUNKS, NZ)),
        dma((1 + CHUNKS,)),
    ]
    hidden, s4, n4 = pl.pallas_call(
        kernel,
        out_shape=(
            jax.ShapeDtypeStruct((targets, hid), BF16),
            jax.ShapeDtypeStruct((NZ, s_rows, LANES), BF16),
            jax.ShapeDtypeStruct((NY, n_rows, LANES), BF16),
        ),
        in_specs=[hbm] * 11,
        out_specs=(hbm,) * 3,
        scratch_shapes=scratch,
        compiler_params=pltpu.CompilerParams(
            collective_id=0, has_side_effects=True, vmem_limit_bytes=VMEM_LIMIT
        ),
        cost_estimate=pl.CostEstimate(flops=300_000_000, bytes_accessed=4_000_000, transcendentals=65536),
    )(
        table.T, node_ids.reshape(NY, 1, NZ * TILE), tiles, tile_rows, tile_cols,
        tile_count, seed_count, w_self, w_neigh, bias.reshape(1, hid), cotangent,
    )
    hidden, grad_self, grad_neigh, grad_bias = pl.pallas_call(
        finish,
        out_shape=(
            jax.ShapeDtypeStruct((targets, hid), BF16),
            jax.ShapeDtypeStruct(w_self.shape, F32),
            jax.ShapeDtypeStruct(w_neigh.shape, F32),
            jax.ShapeDtypeStruct((1, hid), F32),
        ),
        in_specs=[hbm] * 3,
        out_specs=(hbm,) * 4,
        scratch_shapes=[
            vmem((targets, hid), BF16), vmem((NZ, s_rows, LANES), BF16), vmem((NY, n_rows, LANES), BF16),
            vmem(w_self.shape, F32), vmem(w_neigh.shape, F32), vmem((1, hid), F32), dma((5,)), dma((4,)),
        ],
    )(hidden, s4, n4)
    return hidden, grad_self, grad_neigh, grad_bias.reshape(hid)


def solution(mesh):
    placed = (
        P("dp", "feat"),
        P("dp"),
        P("dp", None, None),
        P("dp"),
        P("dp"),
        P("dp"),
        P("dp"),
        P("feat", None),
        P("feat", None),
        P("feat"),
        P("dp", "feat"),
    )
    return jax.shard_map(
        on_device,
        mesh=mesh,
        in_specs=placed,
        out_specs=(P("dp", "feat"), P("feat", None), P("feat", None), P("feat")),
        check_vma=False,
    )
```

```python
import jax
import jax.numpy as jnp
from jax import lax
from jax.experimental import pallas as pl
from jax.experimental.pallas import tpu as pltpu
from jax.sharding import PartitionSpec as P

MESH = pl.DeviceIdType.MESH
F32 = jnp.float32
BF16 = jnp.bfloat16
NY, NZ, NX, NF = 8, 8, 4, 8
NDP = NY * NZ
BLK = 128
LANES = 128
VMEM_LIMIT = 60 * 1024 * 1024
TILE = 16


RING = (4, 5, 3, 6, 2, 7, 1)


def hops(offset):
    return min(offset[0], NY - offset[0]) + min(offset[1], NZ - offset[1])


FARTHEST = sorted(((a, b) for a in range(NY) for b in range(NZ) if a or b), key=lambda o: (-hops(o), o))
CHIPS = (2, 1, 3)
CHUNK_ROWS = ((0, 64, False), (112, 160, True), (64, 112, False), (160, 208, True))
CHUNKS = len(CHUNK_ROWS)
HALVES = 2


def dot(a, b):
    return jnp.dot(a, b, preferred_element_type=F32)


def dot_t(a, b):
    return lax.dot_general(a, b, (((1,), (1,)), ((), ())), preferred_element_type=F32)


def kernel(
    table_hbm, ids_hbm, tiles_hbm, rows_hbm, cols_hbm, count_hbm, seed_hbm, ws_hbm, wn_hbm, bias_hbm, cot_hbm,
    hidden_hbm, s_hbm, n_hbm,
    table_f, table_b, tiles_i, tiles_f, ws_f, wn_f, w_b, w_p, cot_v, bias_v, rows_s, cols_s, count_s, seed_s,
    ids_v, ids_y, ids_buf, rows_send, rows_buf, adj, x_b, x_p, xt_b,
    q_own, p_send, p_recv, sl_all, hid_v,
    *rest,
):
    pieces, rest = rest[:5 * CHUNKS], rest[5 * CHUNKS:]
    (
        loc_sem, ids_ss, idy_rs, idz_rs, rows_ss, rows_rs, q_ss, q_rs, f_ss, send_sem, p_rs, sl_rs, first_rs, second_rs, third_rs,
        out_sem,
    ) = rest
    me = lax.axis_index("dp")
    feat = lax.axis_index("feat")
    y = me // NZ
    z = me % NZ
    x = feat // 2
    core = feat % 2
    fcols = table_f.shape[0]
    mate = x * 2 + 1 - core
    targets = cot_v.shape[0]

    def dp_of(yy, zz):
        return yy * NZ + zz

    own_ids = pltpu.make_async_copy(ids_hbm, ids_v, loc_sem.at[0])
    get_table = pltpu.make_async_copy(table_hbm, table_f, loc_sem.at[1])
    get_ws = pltpu.make_async_copy(ws_hbm, ws_f, loc_sem.at[2])
    get_wn = pltpu.make_async_copy(wn_hbm, wn_f, loc_sem.at[3])
    get_tiles = pltpu.make_async_copy(tiles_hbm, tiles_i, loc_sem.at[4])
    get_cot = pltpu.make_async_copy(cot_hbm, cot_v, loc_sem.at[5])
    small = [
        pltpu.make_async_copy(src, dst, loc_sem.at[6 + n])
        for n, (src, dst) in enumerate((
            (rows_hbm, rows_s), (cols_hbm, cols_s), (count_hbm, count_s), (seed_hbm, seed_s), (bias_hbm, bias_v),
        ))
    ]
    own_ids.start()

    barrier = pltpu.get_barrier_semaphore()

    for k in RING:
        pl.semaphore_signal(barrier, inc=1, device_id=(dp_of((y + k) % NY, z), feat), device_id_type=MESH)
    for k in RING:
        pl.semaphore_signal(barrier, inc=1, device_id=(dp_of(y, (z + k) % NZ), feat), device_id_type=MESH)
    for k in CHIPS:
        pl.semaphore_signal(barrier, inc=1, device_id=(me, (x + k) % NX * 2 + core), device_id_type=MESH)
    pl.semaphore_signal(barrier, inc=1, device_id=(me, mate), device_id_type=MESH)
    pl.semaphore_wait(barrier, NZ - 1 + NY - 1 + NX)

    own_ids.wait()
    for k in RING:
        yy = (y + k) % NY
        pltpu.make_async_remote_copy(
            ids_v.at[yy], ids_y.at[y], ids_ss.at[0], idy_rs,
            device_id=(dp_of(yy, z), feat), device_id_type=MESH,
        ).start()
    get_table.start()
    ids_y[y] = ids_v[y]
    pltpu.make_async_copy(ids_y.at[pl.ds(0, NY - 1)], ids_y.at[pl.ds(0, NY - 1)], idy_rs).wait()
    for k in RING:
        pltpu.make_async_remote_copy(
            ids_y, ids_buf.at[z], ids_ss.at[1], idz_rs,
            device_id=(dp_of(y, (z + k) % NZ), feat), device_id_type=MESH,
        ).start()
    ids_buf[z] = ids_y[...]

    get_table.wait()
    table_b[...] = table_f[...].astype(BF16)
    pltpu.make_async_copy(ids_buf.at[pl.ds(0, NZ - 1)], ids_buf.at[pl.ds(0, NZ - 1)], idz_rs).wait()

    lane = lax.broadcasted_iota(jnp.int32, (NZ, TILE, LANES), 2)
    slot = lax.broadcasted_iota(jnp.int32, (NZ, TILE, LANES), 1)
    mine = lane == z * TILE + slot
    table_rows = table_b.shape[1]
    row_of = lax.broadcasted_iota(jnp.int32, (NZ * TILE, table_rows), 1)

    def gather(step, c):
        pair = ((y + 4 - step) % NY, (y + 5 + step) % NY)
        for yy in pair:
            asked = ids_buf[:, yy].astype(F32)
            picked = jnp.where(mine, jnp.broadcast_to(asked, (NZ, TILE, LANES)), 0.0)
            column = jnp.sum(picked.reshape(NZ * TILE, LANES), axis=1, keepdims=True).astype(jnp.int32)
            hot = jnp.where(column == row_of, 1.0, 0.0).astype(BF16)
            found = dot_t(hot, table_b[...]).astype(BF16)
            rows_send[pl.ds(yy * NZ, NZ)] = found.reshape(NZ, TILE, fcols)
        return c

    def send_rows(chosen):
        for dy, dz in chosen:
            to = dp_of((y + dy) % NY, (z + dz) % NZ)
            pltpu.make_async_remote_copy(
                rows_send.at[to], rows_buf.at[me], rows_ss, rows_rs,
                device_id=(to, feat), device_id_type=MESH,
            ).start()

    lax.fori_loop(0, 2, gather, 0)
    early = [o for o in FARTHEST if o[0] in (3, 4, 5, 6) and hops(o) > 5]
    send_rows(early)
    lax.fori_loop(2, NY // 2, gather, 0)
    send_rows([o for o in FARTHEST if o not in early])
    get_ws.start()
    get_wn.start()
    get_tiles.start()
    for copy in small:
        copy.start()
    get_cot.start()
    rows_buf[me] = rows_send[me]

    get_ws.wait()
    get_wn.wait()
    w_b[...] = jnp.zeros_like(w_b)
    x_b[...] = jnp.zeros_like(x_b)
    for c in range(NX):
        for co in range(2):
            at = (c * 2 + co) * LANES
            w_b[co, c, :fcols] = ws_f[:, at:at + LANES].astype(BF16)
            w_b[co, c, LANES:LANES + fcols] = wn_f[:, at:at + LANES].astype(BF16)
    w_copy = pltpu.make_async_remote_copy(
        w_b.at[1 - core], w_p, q_ss.at[0], q_rs.at[0], device_id=(me, mate), device_id_type=MESH
    )
    w_copy.start()
    get_tiles.wait()
    tiles_f[...] = tiles_i[...].astype(F32)
    n_slots = tiles_f.shape[0]
    for copy in small:
        copy.wait()
    col_blocks = adj.shape[1] // BLK

    def place(i, c):
        r = i // col_blocks
        q = i % col_blocks
        total = jnp.zeros((BLK, BLK), F32)
        for k in range(n_slots):
            on = (rows_s[k] == r) & (cols_s[k] == q) & (k < count_s[0])
            total = total + tiles_f[k] * jnp.where(on, 1.0, 0.0)
        adj[pl.ds(pl.multiple_of(r * BLK, BLK), BLK), pl.ds(pl.multiple_of(q * BLK, BLK), BLK)] = total.astype(BF16)
        return c

    lax.fori_loop(0, (targets // BLK) * col_blocks, place, 0)
    degree = jnp.sum(adj[...].astype(F32), axis=1, keepdims=True)
    scale = 1.0 / jnp.maximum(degree, 1.0)
    get_cot.wait()
    w_copy.wait_recv()

    pltpu.make_async_copy(rows_buf.at[pl.ds(0, NDP - 1)], rows_buf.at[pl.ds(0, NDP - 1)], rows_rs).wait()
    sampled = rows_buf[...].reshape(NDP * TILE, fcols)
    self_rows = sampled[:targets]
    x_b[0, :, :fcols] = self_rows
    x_copies = [
        pltpu.make_async_remote_copy(
            x_b.at[n], x_p.at[n], q_ss.at[1 + n], q_rs.at[1 + n], device_id=(me, mate), device_id_type=MESH
        )
        for n in range(2)
    ]
    x_copies[0].start()
    neigh = dot(adj[...], sampled) * scale
    x_b[1, :, :fcols] = neigh.astype(BF16)
    x_copies[1].start()

    both = jnp.concatenate([x_b[0], x_b[1]], axis=1)
    for k in CHIPS + (0,):
        chip = (x + k) % NX
        q_own[chip] = dot(both, w_b[core, chip])
    for copy in x_copies:
        copy.wait_recv()
    other = jnp.concatenate([x_p[0], x_p[1]], axis=1)
    half = targets // HALVES
    for h in range(HALVES):
        low = h * half
        for k in CHIPS:
            chip = (x + k) % NX
            own = q_own[chip, low:low + half]
            p_send[h, chip] = (own + dot(other[low:low + half], w_p[chip])).astype(BF16)
            pltpu.make_async_remote_copy(
                p_send.at[h, chip], p_recv.at[h, x], send_sem.at[3 * CHUNKS + h], p_rs.at[h, x],
                device_id=(me, chip * 2 + core), device_id_type=MESH,
            ).start()
    preact = q_own[x] + dot(other, w_p[x]) + bias_v[...]

    xs_t = self_rows.astype(F32).T
    xn_t = neigh.T
    ones = jnp.where(lax.broadcasted_iota(jnp.int32, (TILE, targets), 0) == 0, 1.0, 0.0)
    xt_b[:fcols] = xs_t.astype(BF16)
    xt_b[fcols:fcols + TILE] = ones.astype(BF16)
    xt_b[fcols + TILE:] = xn_t.astype(BF16)

    def slope_copy(which, h, sem, to):
        return pltpu.make_async_remote_copy(
            sl_all.at[which, h], sl_all.at[which, h], sem, sl_rs.at[which, h],
            device_id=(me, to), device_id_type=MESH,
        )

    def activate(h):
        low = h * half
        total = preact[low:low + half]
        for k in (1, 3, 2):
            frm = (x + k) % NX
            pltpu.make_async_copy(p_recv.at[h, frm], p_recv.at[h, frm], p_rs.at[h, frm]).wait()
            total = total + p_recv[h, frm].astype(F32)
        row = low + lax.broadcasted_iota(jnp.int32, (half, LANES), 0)
        alive = jnp.where(row < seed_s[0], 1.0, 0.0)
        sigma = jax.nn.sigmoid(total)
        slope = cot_v[low:low + half].astype(F32) * alive * sigma * (1.0 + total * (1.0 - sigma))
        sl_all[feat, h] = slope.astype(BF16)
        for k in CHIPS:
            slope_copy(feat, h, send_sem.at[3 * CHUNKS + HALVES + h], (x + k) % NX * 2 + core).start()
        slope_copy(feat, h, f_ss.at[0, h], mate).start()
        hid_v[low:low + half] = (total * sigma * alive).astype(BF16)

    for h in range(HALVES):
        activate(h)
    put_hidden = pltpu.make_async_copy(hid_v, hidden_hbm, out_sem.at[0])
    put_hidden.start()

    def line(across, k):
        if across:
            return dp_of((y + k) % NY, z)
        return dp_of(y, (z + k) % NZ)

    class Chunk:
        def __init__(self, n):
            self.low, self.high, self.across = CHUNK_ROWS[n]
            self.send, self.recv, self.own, self.second, self.total = pieces[5 * n:5 * n + 5]
            self.here, self.there = (y, z) if self.across else (z, y)
            self.n = n
            base = 0 if self.low < s_rows else s_rows
            self.out = (n_hbm if self.across else s_hbm).at[:, pl.ds(self.low - base, self.high - self.low)]

        def first(self, at, grad):
            part = grad[self.low:self.high]

            @pl.when(at == self.here)
            def _():
                self.own[...] = part

            @pl.when(at != self.here)
            def _():
                self.send[at] = part.astype(BF16)
                to = dp_of(at, z) if self.across else dp_of(y, at)
                pltpu.make_async_remote_copy(
                    self.send.at[at], self.recv.at[self.here], send_sem.at[self.n], first_rs.at[self.n, self.here],
                    device_id=(to, feat), device_id_type=MESH,
                ).start()

        def add_first(self):
            total = self.own[...]
            for k in RING:
                frm = (self.here - k + NZ) % NZ
                pltpu.make_async_copy(self.recv.at[frm], self.recv.at[frm], first_rs.at[self.n, frm]).wait()
                total = total + self.recv[frm].astype(F32)
            self.second[self.there] = total.astype(BF16)
            for k in RING:
                pltpu.make_async_remote_copy(
                    self.second.at[self.there], self.second.at[self.there],
                    send_sem.at[CHUNKS + self.n], second_rs.at[self.n, self.there],
                    device_id=(line(not self.across, k), feat), device_id_type=MESH,
                ).start()

        def add_second(self):
            for k in RING:
                frm = (self.there - k + NZ) % NZ
                pltpu.make_async_copy(self.second.at[frm], self.second.at[frm], second_rs.at[self.n, frm]).wait()
            total = self.second[0].astype(F32)
            for n in range(1, NZ):
                total = total + self.second[n].astype(F32)
            self.total[...] = total.astype(BF16)
            for k in RING:
                pltpu.make_async_remote_copy(
                    self.total, self.out.at[self.here], send_sem.at[2 * CHUNKS + self.n], third_rs.at[self.n, self.here],
                    device_id=(line(self.across, k), feat), device_id_type=MESH,
                ).start()
            self.keep().start()

        def keep(self):
            return pltpu.make_async_copy(self.total, self.out.at[self.here], out_sem.at[1 + self.n])

        def finish(self):
            for k in RING:
                frm = (self.here - k + NZ) % NZ
                pltpu.make_async_copy(self.out.at[frm], self.out.at[frm], third_rs.at[self.n, frm]).wait()
            self.keep().wait()

    s_rows = fcols + TILE
    chunks = [Chunk(n) for n in range(CHUNKS)]

    def first(block):
        grad = dot(xt_b[...], sl_all[block].reshape(targets, LANES))
        for chunk in chunks:
            chunk.first(block // 2 + block % 2 * NX, grad)

    def wait_slope(which, h):
        pltpu.make_async_copy(sl_all.at[which, h], sl_all.at[which, h], sl_rs.at[which, h]).wait()

    first(feat)
    for h in range(HALVES):
        wait_slope(mate, h)
    first(mate)
    for n, k in enumerate((1, 3, 2)):
        direct = (x + k) % NX * 2 + core
        passed = (x + k) % NX * 2 + 1 - core
        for h in range(HALVES):
            wait_slope(direct, h)
            slope_copy(direct, h, f_ss.at[1 + n, h], mate).start()
        first(direct)
        for h in range(HALVES):
            wait_slope(passed, h)
        first(passed)

    for chunk in chunks:
        chunk.add_first()
    for chunk in chunks:
        chunk.add_second()
    for chunk in chunks:
        chunk.finish()
    put_hidden.wait()

    def sent(buf, count, sem):
        pltpu.make_async_copy(buf.at[pl.ds(0, count)], buf.at[pl.ds(0, count)], sem).wait()

    sent(ids_y, NY - 1, ids_ss.at[0])
    sent(ids_buf, NZ - 1, ids_ss.at[1])
    sent(rows_send, NDP - 1, rows_ss)
    for h in range(HALVES):
        sent(p_send.at[h], NX - 1, send_sem.at[3 * CHUNKS + h])
        sent(p_send.at[h], NX - 1, send_sem.at[3 * CHUNKS + HALVES + h])
    for chunk in chunks:
        sent(chunk.send, NZ - 1, send_sem.at[chunk.n])
        sent(chunk.second, NZ - 1, send_sem.at[CHUNKS + chunk.n])
        sent(chunk.send, NZ - 1, send_sem.at[2 * CHUNKS + chunk.n])
    w_copy.wait_send()
    for copy in x_copies:
        copy.wait_send()
    for c in range(NX):
        for h in range(HALVES):
            pltpu.make_async_copy(sl_all.at[c, h], sl_all.at[c, h], f_ss.at[c, h]).wait()


def finish(
    hidden_in, s_in, n_in, hidden_ref, gself_ref, gneigh_ref, gbias_ref, h_v, s_v, n_v, gs_v, gn_v, gb_v, in_sem, out_sem
):
    fcols = gs_v.shape[0]
    gets = []
    for n, (src, dst) in enumerate(((s_in, s_v), (n_in, n_v))):
        for part in range(2):
            rows = pl.ds(part * NX, NX)
            gets.append(pltpu.make_async_copy(src.at[rows], dst.at[rows], in_sem.at[n * 2 + part]))
    for copy in gets:
        copy.start()
    get_hidden = pltpu.make_async_copy(hidden_in, h_v, in_sem.at[4])
    get_hidden.start()
    puts = []

    def put(src, dst):
        puts.append(pltpu.make_async_copy(src, dst, out_sem.at[len(puts)]))
        puts[-1].start()

    feat = lax.axis_index("feat")
    for src, dst, base, out in ((s_v, gs_v, 0, gself_ref), (n_v, gn_v, 2, gneigh_ref)):
        for part in range(2):
            gets[base + part].wait()
            for t in range(part * NX, part * NX + NX):
                c = (t % NX) * 2 + t // NX
                dst[:, c * LANES:(c + 1) * LANES] = src[t][:fcols].astype(F32)
        if base == 0:
            gb_v[...] = s_v[feat // 2 + feat % 2 * NX][fcols:fcols + TILE].astype(F32)[:1]
            put(gb_v, gbias_ref)
        put(dst, out)
        if base == 0:
            get_hidden.wait()
            put(h_v, hidden_ref)
    for copy in puts:
        copy.wait()


def on_device(table, node_ids, tiles, tile_rows, tile_cols, tile_count, seed_count, w_self, w_neigh, bias, cotangent):
    fcols = table.shape[1]
    hidden_all = w_self.shape[1]
    targets, hid = cotangent.shape
    s_rows, n_rows = fcols + TILE, fcols
    vmem = pltpu.VMEM
    dma = pltpu.SemaphoreType.DMA
    hbm = pl.BlockSpec(memory_space=pl.ANY)
    scratch = [
        vmem(table.shape[::-1], F32),
        vmem(table.shape[::-1], BF16),
        vmem(tiles.shape, jnp.int32),
        vmem(tiles.shape, F32),
        vmem(w_self.shape, F32),
        vmem(w_neigh.shape, F32),
        vmem((2, NX, 2 * LANES, LANES), BF16),
        vmem((NX, 2 * LANES, LANES), BF16),
        vmem(cotangent.shape, BF16),
        vmem((1, hid), F32),
        pltpu.SMEM(tile_rows.shape, jnp.int32),
        pltpu.SMEM(tile_cols.shape, jnp.int32),
        pltpu.SMEM(tile_count.shape, jnp.int32),
        pltpu.SMEM(seed_count.shape, jnp.int32),
        vmem((NY, 1, LANES), jnp.int32),
        vmem((NY, 1, LANES), jnp.int32),
        vmem((NZ, NY, 1, LANES), jnp.int32),
        vmem((NDP, TILE, fcols), BF16),
        vmem((NDP, TILE, fcols), BF16),
        vmem((targets, NDP * TILE), BF16),
        vmem((2, targets, LANES), BF16),
        vmem((2, targets, LANES), BF16),
        vmem((s_rows + n_rows, targets), BF16),
        vmem((NX, targets, hid), F32),
        vmem((HALVES, NX, targets // HALVES, hid), BF16),
        vmem((HALVES, NX, targets // HALVES, hid), BF16),
        vmem((NF, HALVES, targets // HALVES, hid), BF16),
        vmem((targets, hid), BF16),
    ]
    for low, high, _ in CHUNK_ROWS:
        rows = high - low
        scratch += [
            vmem((NZ, rows, LANES), BF16),
            vmem((NZ, rows, LANES), BF16),
            vmem((rows, LANES), F32),
            vmem((NZ, rows, LANES), BF16),
            vmem((rows, LANES), BF16),
        ]
    scratch += [
        dma((11,)),
        dma((2,)), dma, dma, dma, dma,
        dma((3,)), dma((3,)), dma((NX, HALVES)),
        dma((3 * CHUNKS + 2 * HALVES,)),
        dma((HALVES, NX)), dma((NF, HALVES)),
        dma((CHUNKS, NZ)), dma((CHUNKS, NZ)), dma((CHUNKS, NZ)),
        dma((1 + CHUNKS,)),
    ]
    hidden, s4, n4 = pl.pallas_call(
        kernel,
        out_shape=(
            jax.ShapeDtypeStruct((targets, hid), BF16),
            jax.ShapeDtypeStruct((NZ, s_rows, LANES), BF16),
            jax.ShapeDtypeStruct((NY, n_rows, LANES), BF16),
        ),
        in_specs=[hbm] * 11,
        out_specs=(hbm,) * 3,
        scratch_shapes=scratch,
        compiler_params=pltpu.CompilerParams(
            collective_id=0, has_side_effects=True, vmem_limit_bytes=VMEM_LIMIT
        ),
        cost_estimate=pl.CostEstimate(flops=300_000_000, bytes_accessed=4_000_000, transcendentals=65536),
    )(
        table.T, node_ids.reshape(NY, 1, NZ * TILE), tiles, tile_rows, tile_cols,
        tile_count, seed_count, w_self, w_neigh, bias.reshape(1, hid), cotangent,
    )
    hidden, grad_self, grad_neigh, grad_bias = pl.pallas_call(
        finish,
        out_shape=(
            jax.ShapeDtypeStruct((targets, hid), BF16),
            jax.ShapeDtypeStruct(w_self.shape, F32),
            jax.ShapeDtypeStruct(w_neigh.shape, F32),
            jax.ShapeDtypeStruct((1, hid), F32),
        ),
        in_specs=[hbm] * 3,
        out_specs=(hbm,) * 4,
        scratch_shapes=[
            vmem((targets, hid), BF16), vmem((NZ, s_rows, LANES), BF16), vmem((NY, n_rows, LANES), BF16),
            vmem(w_self.shape, F32), vmem(w_neigh.shape, F32), vmem((1, hid), F32), dma((5,)), dma((4,)),
        ],
    )(hidden, s4, n4)
    return hidden, grad_self, grad_neigh, grad_bias.reshape(hid)


def solution(mesh):
    placed = (
        P("dp", "feat"),
        P("dp"),
        P("dp", None, None),
        P("dp"),
        P("dp"),
        P("dp"),
        P("dp"),
        P("feat", None),
        P("feat", None),
        P("feat"),
        P("dp", "feat"),
    )
    return jax.shard_map(
        on_device,
        mesh=mesh,
        in_specs=placed,
        out_specs=(P("dp", "feat"), P("feat", None), P("feat", None), P("feat")),
        check_vma=False,
    )
```

```python
import jax
import jax.numpy as jnp
from jax import lax
from jax.experimental import pallas as pl
from jax.experimental.pallas import tpu as pltpu
from jax.sharding import PartitionSpec as P

MESH = pl.DeviceIdType.MESH
F32 = jnp.float32
BF16 = jnp.bfloat16
NY, NZ, NX, NF = 8, 8, 4, 8
NDP = NY * NZ
BLK = 128
LANES = 128
VMEM_LIMIT = 60 * 1024 * 1024
TILE = 16


RING = (4, 5, 3, 6, 2, 7, 1)


def hops(offset):
    return min(offset[0], NY - offset[0]) + min(offset[1], NZ - offset[1])


FARTHEST = sorted(((a, b) for a in range(NY) for b in range(NZ) if a or b), key=lambda o: (-hops(o), o))
CHIPS = (2, 1, 3)
CHUNK_ROWS = ((0, 64, False), (112, 160, True), (64, 112, False), (160, 208, True))
CHUNKS = len(CHUNK_ROWS)
HALVES = 2


def dot(a, b):
    return jnp.dot(a, b, preferred_element_type=F32)


def dot_t(a, b):
    return lax.dot_general(a, b, (((1,), (1,)), ((), ())), preferred_element_type=F32)


def kernel(
    table_hbm, ids_hbm, tiles_hbm, rows_hbm, cols_hbm, count_hbm, seed_hbm, ws_hbm, wn_hbm, bias_hbm, cot_hbm,
    hidden_hbm, s_hbm, n_hbm,
    table_f, table_b, tiles_i, tiles_f, ws_f, wn_f, w_b, w_p, cot_v, bias_v, rows_s, cols_s, count_s, seed_s,
    ids_v, ids_y, ids_buf, rows_send, rows_buf, adj, x_b, x_p, xt_b,
    q_own, p_send, p_recv, sl_all, hid_v,
    *rest,
):
    pieces, rest = rest[:5 * CHUNKS], rest[5 * CHUNKS:]
    (
        loc_sem, ids_ss, idy_rs, idz_rs, rows_ss, rows_rs, q_ss, q_rs, f_ss, send_sem, p_rs, sl_rs, first_rs, second_rs, third_rs,
        out_sem,
    ) = rest
    me = lax.axis_index("dp")
    feat = lax.axis_index("feat")
    y = me // NZ
    z = me % NZ
    x = feat // 2
    core = feat % 2
    fcols = table_f.shape[0]
    mate = x * 2 + 1 - core
    targets = cot_v.shape[0]

    def dp_of(yy, zz):
        return yy * NZ + zz

    own_ids = pltpu.make_async_copy(ids_hbm, ids_v, loc_sem.at[0])
    get_table = pltpu.make_async_copy(table_hbm, table_f, loc_sem.at[1])
    get_ws = pltpu.make_async_copy(ws_hbm, ws_f, loc_sem.at[2])
    get_wn = pltpu.make_async_copy(wn_hbm, wn_f, loc_sem.at[3])
    get_tiles = pltpu.make_async_copy(tiles_hbm, tiles_i, loc_sem.at[4])
    get_cot = pltpu.make_async_copy(cot_hbm, cot_v, loc_sem.at[5])
    small = [
        pltpu.make_async_copy(src, dst, loc_sem.at[6 + n])
        for n, (src, dst) in enumerate((
            (rows_hbm, rows_s), (cols_hbm, cols_s), (count_hbm, count_s), (seed_hbm, seed_s), (bias_hbm, bias_v),
        ))
    ]
    own_ids.start()

    barrier = pltpu.get_barrier_semaphore()

    for k in RING:
        pl.semaphore_signal(barrier, inc=1, device_id=(dp_of((y + k) % NY, z), feat), device_id_type=MESH)
    for k in RING:
        pl.semaphore_signal(barrier, inc=1, device_id=(dp_of(y, (z + k) % NZ), feat), device_id_type=MESH)
    for k in CHIPS:
        pl.semaphore_signal(barrier, inc=1, device_id=(me, (x + k) % NX * 2 + core), device_id_type=MESH)
    pl.semaphore_signal(barrier, inc=1, device_id=(me, mate), device_id_type=MESH)
    pl.semaphore_wait(barrier, NZ - 1 + NY - 1 + NX)

    own_ids.wait()
    for k in RING:
        yy = (y + k) % NY
        pltpu.make_async_remote_copy(
            ids_v.at[yy], ids_y.at[y], ids_ss.at[0], idy_rs,
            device_id=(dp_of(yy, z), feat), device_id_type=MESH,
        ).start()
    get_table.start()
    get_ws.start()
    get_wn.start()
    get_tiles.start()
    for copy in small:
        copy.start()
    get_cot.start()
    ids_y[y] = ids_v[y]
    pltpu.make_async_copy(ids_y.at[pl.ds(0, NY - 1)], ids_y.at[pl.ds(0, NY - 1)], idy_rs).wait()
    for k in RING:
        pltpu.make_async_remote_copy(
            ids_y, ids_buf.at[z], ids_ss.at[1], idz_rs,
            device_id=(dp_of(y, (z + k) % NZ), feat), device_id_type=MESH,
        ).start()
    ids_buf[z] = ids_y[...]

    get_table.wait()
    table_b[...] = table_f[...].astype(BF16)
    pltpu.make_async_copy(ids_buf.at[pl.ds(0, NZ - 1)], ids_buf.at[pl.ds(0, NZ - 1)], idz_rs).wait()

    lane = lax.broadcasted_iota(jnp.int32, (NZ, TILE, LANES), 2)
    slot = lax.broadcasted_iota(jnp.int32, (NZ, TILE, LANES), 1)
    mine = lane == z * TILE + slot
    table_rows = table_b.shape[1]
    row_of = lax.broadcasted_iota(jnp.int32, (NZ * TILE, table_rows), 1)

    def gather(step, c):
        pair = ((y + 4 - step) % NY, (y + 5 + step) % NY)
        for yy in pair:
            asked = ids_buf[:, yy].astype(F32)
            picked = jnp.where(mine, jnp.broadcast_to(asked, (NZ, TILE, LANES)), 0.0)
            column = jnp.sum(picked.reshape(NZ * TILE, LANES), axis=1, keepdims=True).astype(jnp.int32)
            hot = jnp.where(column == row_of, 1.0, 0.0).astype(BF16)
            found = dot_t(hot, table_b[...]).astype(BF16)
            rows_send[pl.ds(yy * NZ, NZ)] = found.reshape(NZ, TILE, fcols)
        return c

    def send_rows(chosen):
        for dy, dz in chosen:
            to = dp_of((y + dy) % NY, (z + dz) % NZ)
            pltpu.make_async_remote_copy(
                rows_send.at[to], rows_buf.at[me], rows_ss, rows_rs,
                device_id=(to, feat), device_id_type=MESH,
            ).start()

    lax.fori_loop(0, 2, gather, 0)
    early = [o for o in FARTHEST if o[0] in (3, 4, 5, 6) and hops(o) > 5]
    send_rows(early)
    lax.fori_loop(2, NY // 2, gather, 0)
    send_rows([o for o in FARTHEST if o not in early])
    rows_buf[me] = rows_send[me]

    get_ws.wait()
    get_wn.wait()
    w_b[...] = jnp.zeros_like(w_b)
    x_b[...] = jnp.zeros_like(x_b)
    for c in range(NX):
        for co in range(2):
            at = (c * 2 + co) * LANES
            w_b[co, c, :fcols] = ws_f[:, at:at + LANES].astype(BF16)
            w_b[co, c, LANES:LANES + fcols] = wn_f[:, at:at + LANES].astype(BF16)
    w_copy = pltpu.make_async_remote_copy(
        w_b.at[1 - core], w_p, q_ss.at[0], q_rs.at[0], device_id=(me, mate), device_id_type=MESH
    )
    w_copy.start()
    get_tiles.wait()
    tiles_f[...] = tiles_i[...].astype(F32)
    n_slots = tiles_f.shape[0]
    for copy in small:
        copy.wait()
    col_blocks = adj.shape[1] // BLK

    def place(i, c):
        r = i // col_blocks
        q = i % col_blocks
        total = jnp.zeros((BLK, BLK), F32)
        for k in range(n_slots):
            on = (rows_s[k] == r) & (cols_s[k] == q) & (k < count_s[0])
            total = total + tiles_f[k] * jnp.where(on, 1.0, 0.0)
        adj[pl.ds(pl.multiple_of(r * BLK, BLK), BLK), pl.ds(pl.multiple_of(q * BLK, BLK), BLK)] = total.astype(BF16)
        return c

    lax.fori_loop(0, (targets // BLK) * col_blocks, place, 0)
    degree = jnp.sum(adj[...].astype(F32), axis=1, keepdims=True)
    scale = 1.0 / jnp.maximum(degree, 1.0)
    get_cot.wait()
    w_copy.wait_recv()

    pltpu.make_async_copy(rows_buf.at[pl.ds(0, NDP - 1)], rows_buf.at[pl.ds(0, NDP - 1)], rows_rs).wait()
    sampled = rows_buf[...].reshape(NDP * TILE, fcols)
    self_rows = sampled[:targets]
    neigh = dot(adj[...], sampled) * scale
    x_b[0, :, :fcols] = self_rows
    x_b[1, :, :fcols] = neigh.astype(BF16)
    x_copy = pltpu.make_async_remote_copy(
        x_b, x_p, q_ss.at[1], q_rs.at[1], device_id=(me, mate), device_id_type=MESH
    )
    x_copy.start()

    both = jnp.concatenate([x_b[0], x_b[1]], axis=1)
    for k in CHIPS + (0,):
        chip = (x + k) % NX
        q_own[chip] = dot(both, w_b[core, chip])
    x_copy.wait_recv()
    other = jnp.concatenate([x_p[0], x_p[1]], axis=1)
    half = targets // HALVES
    for h in range(HALVES):
        low = h * half
        for k in CHIPS:
            chip = (x + k) % NX
            own = q_own[chip, low:low + half]
            p_send[h, chip] = (own + dot(other[low:low + half], w_p[chip])).astype(BF16)
            pltpu.make_async_remote_copy(
                p_send.at[h, chip], p_recv.at[h, x], send_sem.at[3 * CHUNKS + h], p_rs.at[h, x],
                device_id=(me, chip * 2 + core), device_id_type=MESH,
            ).start()
    preact = q_own[x] + dot(other, w_p[x]) + bias_v[...]

    xs_t = self_rows.astype(F32).T
    xn_t = neigh.T
    ones = jnp.where(lax.broadcasted_iota(jnp.int32, (TILE, targets), 0) == 0, 1.0, 0.0)
    xt_b[:fcols] = xs_t.astype(BF16)
    xt_b[fcols:fcols + TILE] = ones.astype(BF16)
    xt_b[fcols + TILE:] = xn_t.astype(BF16)

    def slope_copy(which, h, sem, to):
        return pltpu.make_async_remote_copy(
            sl_all.at[which, h], sl_all.at[which, h], sem, sl_rs.at[which, h],
            device_id=(me, to), device_id_type=MESH,
        )

    def activate(h):
        low = h * half
        total = preact[low:low + half]
        for k in (1, 3, 2):
            frm = (x + k) % NX
            pltpu.make_async_copy(p_recv.at[h, frm], p_recv.at[h, frm], p_rs.at[h, frm]).wait()
            total = total + p_recv[h, frm].astype(F32)
        row = low + lax.broadcasted_iota(jnp.int32, (half, LANES), 0)
        alive = jnp.where(row < seed_s[0], 1.0, 0.0)
        sigma = jax.nn.sigmoid(total)
        slope = cot_v[low:low + half].astype(F32) * alive * sigma * (1.0 + total * (1.0 - sigma))
        sl_all[feat, h] = slope.astype(BF16)
        for k in CHIPS:
            slope_copy(feat, h, send_sem.at[3 * CHUNKS + HALVES + h], (x + k) % NX * 2 + core).start()
        slope_copy(feat, h, f_ss.at[0, h], mate).start()
        hid_v[low:low + half] = (total * sigma * alive).astype(BF16)

    for h in range(HALVES):
        activate(h)
    put_hidden = pltpu.make_async_copy(hid_v, hidden_hbm, out_sem.at[0])
    put_hidden.start()

    def line(across, k):
        if across:
            return dp_of((y + k) % NY, z)
        return dp_of(y, (z + k) % NZ)

    class Chunk:
        def __init__(self, n):
            self.low, self.high, self.across = CHUNK_ROWS[n]
            self.send, self.recv, self.own, self.second, self.total = pieces[5 * n:5 * n + 5]
            self.here, self.there = (y, z) if self.across else (z, y)
            self.n = n
            base = 0 if self.low < s_rows else s_rows
            self.out = (n_hbm if self.across else s_hbm).at[:, pl.ds(self.low - base, self.high - self.low)]

        def first(self, at, grad):
            part = grad[self.low:self.high]

            @pl.when(at == self.here)
            def _():
                self.own[...] = part

            @pl.when(at != self.here)
            def _():
                self.send[at] = part.astype(BF16)
                to = dp_of(at, z) if self.across else dp_of(y, at)
                pltpu.make_async_remote_copy(
                    self.send.at[at], self.recv.at[self.here], send_sem.at[self.n], first_rs.at[self.n, self.here],
                    device_id=(to, feat), device_id_type=MESH,
                ).start()

        def add_first(self):
            total = self.own[...]
            for k in RING:
                frm = (self.here - k + NZ) % NZ
                pltpu.make_async_copy(self.recv.at[frm], self.recv.at[frm], first_rs.at[self.n, frm]).wait()
                total = total + self.recv[frm].astype(F32)
            self.second[self.there] = total.astype(BF16)
            for k in RING:
                pltpu.make_async_remote_copy(
                    self.second.at[self.there], self.second.at[self.there],
                    send_sem.at[CHUNKS + self.n], second_rs.at[self.n, self.there],
                    device_id=(line(not self.across, k), feat), device_id_type=MESH,
                ).start()

        def add_second(self):
            for k in RING:
                frm = (self.there - k + NZ) % NZ
                pltpu.make_async_copy(self.second.at[frm], self.second.at[frm], second_rs.at[self.n, frm]).wait()
            total = self.second[0].astype(F32)
            for n in range(1, NZ):
                total = total + self.second[n].astype(F32)
            self.total[...] = total.astype(BF16)
            for k in RING:
                pltpu.make_async_remote_copy(
                    self.total, self.out.at[self.here], send_sem.at[2 * CHUNKS + self.n], third_rs.at[self.n, self.here],
                    device_id=(line(self.across, k), feat), device_id_type=MESH,
                ).start()
            self.keep().start()

        def keep(self):
            return pltpu.make_async_copy(self.total, self.out.at[self.here], out_sem.at[1 + self.n])

        def finish(self):
            for k in RING:
                frm = (self.here - k + NZ) % NZ
                pltpu.make_async_copy(self.out.at[frm], self.out.at[frm], third_rs.at[self.n, frm]).wait()
            self.keep().wait()

    s_rows = fcols + TILE
    chunks = [Chunk(n) for n in range(CHUNKS)]

    def first(block):
        grad = dot(xt_b[...], sl_all[block].reshape(targets, LANES))
        for chunk in chunks:
            chunk.first(block // 2 + block % 2 * NX, grad)

    def wait_slope(which, h):
        pltpu.make_async_copy(sl_all.at[which, h], sl_all.at[which, h], sl_rs.at[which, h]).wait()

    first(feat)
    for h in range(HALVES):
        wait_slope(mate, h)
    first(mate)
    for n, k in enumerate((1, 3, 2)):
        direct = (x + k) % NX * 2 + core
        passed = (x + k) % NX * 2 + 1 - core
        for h in range(HALVES):
            wait_slope(direct, h)
            slope_copy(direct, h, f_ss.at[1 + n, h], mate).start()
        first(direct)
        for h in range(HALVES):
            wait_slope(passed, h)
        first(passed)

    for chunk in chunks:
        chunk.add_first()
    for chunk in chunks:
        chunk.add_second()
    put_hidden.wait()

    def sent(buf, count, sem):
        pltpu.make_async_copy(buf.at[pl.ds(0, count)], buf.at[pl.ds(0, count)], sem).wait()

    sent(ids_y, NY - 1, ids_ss.at[0])
    sent(ids_buf, NZ - 1, ids_ss.at[1])
    sent(rows_send, NDP - 1, rows_ss)
    for h in range(HALVES):
        sent(p_send.at[h], NX - 1, send_sem.at[3 * CHUNKS + h])
        sent(p_send.at[h], NX - 1, send_sem.at[3 * CHUNKS + HALVES + h])
    for chunk in chunks:
        sent(chunk.send, NZ - 1, send_sem.at[chunk.n])
        sent(chunk.second, NZ - 1, send_sem.at[CHUNKS + chunk.n])
    w_copy.wait_send()
    x_copy.wait_send()
    for c in range(NX):
        for h in range(HALVES):
            pltpu.make_async_copy(sl_all.at[c, h], sl_all.at[c, h], f_ss.at[c, h]).wait()
    for chunk in chunks:
        chunk.finish()
    for chunk in chunks:
        sent(chunk.send, NZ - 1, send_sem.at[2 * CHUNKS + chunk.n])


def finish(
    hidden_in, s_in, n_in, hidden_ref, gself_ref, gneigh_ref, gbias_ref, h_v, s_v, n_v, gs_v, gn_v, gb_v, in_sem, out_sem
):
    fcols = gs_v.shape[0]
    gets = []
    for n, (src, dst) in enumerate(((s_in, s_v), (n_in, n_v))):
        for part in range(2):
            rows = pl.ds(part * NX, NX)
            gets.append(pltpu.make_async_copy(src.at[rows], dst.at[rows], in_sem.at[n * 2 + part]))
    for copy in gets:
        copy.start()
    get_hidden = pltpu.make_async_copy(hidden_in, h_v, in_sem.at[4])
    get_hidden.start()
    puts = []

    def put(src, dst):
        puts.append(pltpu.make_async_copy(src, dst, out_sem.at[len(puts)]))
        puts[-1].start()

    feat = lax.axis_index("feat")
    for src, dst, base, out in ((s_v, gs_v, 0, gself_ref), (n_v, gn_v, 2, gneigh_ref)):
        for part in range(2):
            gets[base + part].wait()
            for t in range(part * NX, part * NX + NX):
                c = (t % NX) * 2 + t // NX
                dst[:, c * LANES:(c + 1) * LANES] = src[t][:fcols].astype(F32)
        if base == 0:
            gb_v[...] = s_v[feat // 2 + feat % 2 * NX][fcols:fcols + TILE].astype(F32)[:1]
            put(gb_v, gbias_ref)
        put(dst, out)
        if base == 0:
            get_hidden.wait()
            put(h_v, hidden_ref)
    for copy in puts:
        copy.wait()


def on_device(table, node_ids, tiles, tile_rows, tile_cols, tile_count, seed_count, w_self, w_neigh, bias, cotangent):
    fcols = table.shape[1]
    hidden_all = w_self.shape[1]
    targets, hid = cotangent.shape
    s_rows, n_rows = fcols + TILE, fcols
    vmem = pltpu.VMEM
    dma = pltpu.SemaphoreType.DMA
    hbm = pl.BlockSpec(memory_space=pl.ANY)
    scratch = [
        vmem(table.shape[::-1], F32),
        vmem(table.shape[::-1], BF16),
        vmem(tiles.shape, jnp.int32),
        vmem(tiles.shape, F32),
        vmem(w_self.shape, F32),
        vmem(w_neigh.shape, F32),
        vmem((2, NX, 2 * LANES, LANES), BF16),
        vmem((NX, 2 * LANES, LANES), BF16),
        vmem(cotangent.shape, BF16),
        vmem((1, hid), F32),
        pltpu.SMEM(tile_rows.shape, jnp.int32),
        pltpu.SMEM(tile_cols.shape, jnp.int32),
        pltpu.SMEM(tile_count.shape, jnp.int32),
        pltpu.SMEM(seed_count.shape, jnp.int32),
        vmem((NY, 1, LANES), jnp.int32),
        vmem((NY, 1, LANES), jnp.int32),
        vmem((NZ, NY, 1, LANES), jnp.int32),
        vmem((NDP, TILE, fcols), BF16),
        vmem((NDP, TILE, fcols), BF16),
        vmem((targets, NDP * TILE), BF16),
        vmem((2, targets, LANES), BF16),
        vmem((2, targets, LANES), BF16),
        vmem((s_rows + n_rows, targets), BF16),
        vmem((NX, targets, hid), F32),
        vmem((HALVES, NX, targets // HALVES, hid), BF16),
        vmem((HALVES, NX, targets // HALVES, hid), BF16),
        vmem((NF, HALVES, targets // HALVES, hid), BF16),
        vmem((targets, hid), BF16),
    ]
    for low, high, _ in CHUNK_ROWS:
        rows = high - low
        scratch += [
            vmem((NZ, rows, LANES), BF16),
            vmem((NZ, rows, LANES), BF16),
            vmem((rows, LANES), F32),
            vmem((NZ, rows, LANES), BF16),
            vmem((rows, LANES), BF16),
        ]
    scratch += [
        dma((11,)),
        dma((2,)), dma, dma, dma, dma,
        dma((2,)), dma((2,)), dma((NX, HALVES)),
        dma((3 * CHUNKS + 2 * HALVES,)),
        dma((HALVES, NX)), dma((NF, HALVES)),
        dma((CHUNKS, NZ)), dma((CHUNKS, NZ)), dma((CHUNKS, NZ)),
        dma((1 + CHUNKS,)),
    ]
    hidden, s4, n4 = pl.pallas_call(
        kernel,
        out_shape=(
            jax.ShapeDtypeStruct((targets, hid), BF16),
            jax.ShapeDtypeStruct((NZ, s_rows, LANES), BF16),
            jax.ShapeDtypeStruct((NY, n_rows, LANES), BF16),
        ),
        in_specs=[hbm] * 11,
        out_specs=(hbm,) * 3,
        scratch_shapes=scratch,
        compiler_params=pltpu.CompilerParams(
            collective_id=0, has_side_effects=True, vmem_limit_bytes=VMEM_LIMIT
        ),
        cost_estimate=pl.CostEstimate(flops=300_000_000, bytes_accessed=4_000_000, transcendentals=65536),
    )(
        table.T, node_ids.reshape(NY, 1, NZ * TILE), tiles, tile_rows, tile_cols,
        tile_count, seed_count, w_self, w_neigh, bias.reshape(1, hid), cotangent,
    )
    hidden, grad_self, grad_neigh, grad_bias = pl.pallas_call(
        finish,
        out_shape=(
            jax.ShapeDtypeStruct((targets, hid), BF16),
            jax.ShapeDtypeStruct(w_self.shape, F32),
            jax.ShapeDtypeStruct(w_neigh.shape, F32),
            jax.ShapeDtypeStruct((1, hid), F32),
        ),
        in_specs=[hbm] * 3,
        out_specs=(hbm,) * 4,
        scratch_shapes=[
            vmem((targets, hid), BF16), vmem((NZ, s_rows, LANES), BF16), vmem((NY, n_rows, LANES), BF16),
            vmem(w_self.shape, F32), vmem(w_neigh.shape, F32), vmem((1, hid), F32), dma((5,)), dma((4,)),
        ],
    )(hidden, s4, n4)
    return hidden, grad_self, grad_neigh, grad_bias.reshape(hid)


def solution(mesh):
    placed = (
        P("dp", "feat"),
        P("dp"),
        P("dp", None, None),
        P("dp"),
        P("dp"),
        P("dp"),
        P("dp"),
        P("feat", None),
        P("feat", None),
        P("feat"),
        P("dp", "feat"),
    )
    return jax.shard_map(
        on_device,
        mesh=mesh,
        in_specs=placed,
        out_specs=(P("dp", "feat"), P("feat", None), P("feat", None), P("feat")),
        check_vma=False,
    )
```

```python
import jax
import jax.numpy as jnp
from jax import lax
from jax.experimental import pallas as pl
from jax.experimental.pallas import tpu as pltpu
from jax.sharding import PartitionSpec as P

MESH = pl.DeviceIdType.MESH
F32 = jnp.float32
BF16 = jnp.bfloat16
NY, NZ, NX, NF = 8, 8, 4, 8
NDP = NY * NZ
BLK = 128
LANES = 128
VMEM_LIMIT = 60 * 1024 * 1024
TILE = 16


RING = (4, 5, 3, 6, 2, 7, 1)


def hops(offset):
    return min(offset[0], NY - offset[0]) + min(offset[1], NZ - offset[1])


FARTHEST = sorted(((a, b) for a in range(NY) for b in range(NZ) if a or b), key=lambda o: (-hops(o), o))
CHIPS = (2, 1, 3)
CHUNK_ROWS = ((0, 64, False), (112, 160, True), (64, 112, False), (160, 208, True))
CHUNKS = len(CHUNK_ROWS)
HALVES = 2


def dot(a, b):
    return jnp.dot(a, b, preferred_element_type=F32)


def dot_t(a, b):
    return lax.dot_general(a, b, (((1,), (1,)), ((), ())), preferred_element_type=F32)


def kernel(
    table_hbm, ids_hbm, tiles_hbm, rows_hbm, cols_hbm, count_hbm, seed_hbm, ws_hbm, wn_hbm, bias_hbm, cot_hbm,
    hidden_hbm, s_hbm, n_hbm,
    table_f, table_b, tiles_i, tiles_f, ws_f, wn_f, w_b, w_p, cot_v, bias_v, rows_s, cols_s, count_s, seed_s,
    ids_v, ids_y, ids_buf, rows_send, rows_buf, adj, x_b, x_p, xt_b,
    q_own, p_send, p_recv, sl_all, hid_v,
    *rest,
):
    pieces, rest = rest[:5 * CHUNKS], rest[5 * CHUNKS:]
    (
        loc_sem, ids_ss, idy_rs, idz_rs, rows_ss, rows_rs, q_ss, q_rs, f_ss, send_sem, p_rs, sl_rs, first_rs, second_rs, third_rs,
        out_sem,
    ) = rest
    me = lax.axis_index("dp")
    feat = lax.axis_index("feat")
    y = me // NZ
    z = me % NZ
    x = feat // 2
    core = feat % 2
    fcols = table_f.shape[0]
    mate = x * 2 + 1 - core
    targets = cot_v.shape[0]

    def dp_of(yy, zz):
        return yy * NZ + zz

    own_ids = pltpu.make_async_copy(ids_hbm, ids_v, loc_sem.at[0])
    get_table = pltpu.make_async_copy(table_hbm, table_f, loc_sem.at[1])
    get_ws = pltpu.make_async_copy(ws_hbm, ws_f, loc_sem.at[2])
    get_wn = pltpu.make_async_copy(wn_hbm, wn_f, loc_sem.at[3])
    get_tiles = pltpu.make_async_copy(tiles_hbm, tiles_i, loc_sem.at[4])
    get_cot = pltpu.make_async_copy(cot_hbm, cot_v, loc_sem.at[5])
    small = [
        pltpu.make_async_copy(src, dst, loc_sem.at[6 + n])
        for n, (src, dst) in enumerate((
            (rows_hbm, rows_s), (cols_hbm, cols_s), (count_hbm, count_s), (seed_hbm, seed_s), (bias_hbm, bias_v),
        ))
    ]
    own_ids.start()

    barrier = pltpu.get_barrier_semaphore()

    for k in RING:
        pl.semaphore_signal(barrier, inc=1, device_id=(dp_of((y + k) % NY, z), feat), device_id_type=MESH)
    for k in RING:
        pl.semaphore_signal(barrier, inc=1, device_id=(dp_of(y, (z + k) % NZ), feat), device_id_type=MESH)
    for k in CHIPS:
        pl.semaphore_signal(barrier, inc=1, device_id=(me, (x + k) % NX * 2 + core), device_id_type=MESH)
    pl.semaphore_signal(barrier, inc=1, device_id=(me, mate), device_id_type=MESH)
    pl.semaphore_wait(barrier, NZ - 1 + NY - 1 + NX)

    own_ids.wait()
    for k in RING:
        yy = (y + k) % NY
        pltpu.make_async_remote_copy(
            ids_v.at[yy], ids_y.at[y], ids_ss.at[0], idy_rs,
            device_id=(dp_of(yy, z), feat), device_id_type=MESH,
        ).start()
    get_table.start()
    get_ws.start()
    get_wn.start()
    get_tiles.start()
    for copy in small:
        copy.start()
    get_cot.start()
    ids_y[y] = ids_v[y]
    pltpu.make_async_copy(ids_y.at[pl.ds(0, NY - 1)], ids_y.at[pl.ds(0, NY - 1)], idy_rs).wait()
    for k in RING:
        pltpu.make_async_remote_copy(
            ids_y, ids_buf.at[z], ids_ss.at[1], idz_rs,
            device_id=(dp_of(y, (z + k) % NZ), feat), device_id_type=MESH,
        ).start()
    ids_buf[z] = ids_y[...]

    get_table.wait()
    table_b[...] = table_f[...].astype(BF16)
    pltpu.make_async_copy(ids_buf.at[pl.ds(0, NZ - 1)], ids_buf.at[pl.ds(0, NZ - 1)], idz_rs).wait()

    lane = lax.broadcasted_iota(jnp.int32, (NZ, TILE, LANES), 2)
    slot = lax.broadcasted_iota(jnp.int32, (NZ, TILE, LANES), 1)
    mine = lane == z * TILE + slot
    table_rows = table_b.shape[1]
    row_of = lax.broadcasted_iota(jnp.int32, (NZ * TILE, table_rows), 1)

    def gather(step, c):
        pair = ((y + 4 - step) % NY, (y + 5 + step) % NY)
        for yy in pair:
            asked = ids_buf[:, yy].astype(F32)
            picked = jnp.where(mine, jnp.broadcast_to(asked, (NZ, TILE, LANES)), 0.0)
            column = jnp.sum(picked.reshape(NZ * TILE, LANES), axis=1, keepdims=True).astype(jnp.int32)
            hot = jnp.where(column == row_of, 1.0, 0.0).astype(BF16)
            found = dot_t(hot, table_b[...]).astype(BF16)
            rows_send[pl.ds(yy * NZ, NZ)] = found.reshape(NZ, TILE, fcols)
        return c

    def send_rows(chosen):
        for dy, dz in chosen:
            to = dp_of((y + dy) % NY, (z + dz) % NZ)
            pltpu.make_async_remote_copy(
                rows_send.at[to], rows_buf.at[me], rows_ss, rows_rs,
                device_id=(to, feat), device_id_type=MESH,
            ).start()

    lax.fori_loop(0, 2, gather, 0)
    early = [o for o in FARTHEST if o[0] in (3, 4, 5, 6) and hops(o) > 5]
    send_rows(early)
    lax.fori_loop(2, NY // 2, gather, 0)
    send_rows([o for o in FARTHEST if o not in early])
    rows_buf[me] = rows_send[me]

    get_ws.wait()
    get_wn.wait()
    w_b[...] = jnp.zeros_like(w_b)
    x_b[...] = jnp.zeros_like(x_b)
    for c in range(NX):
        for co in range(2):
            at = (c * 2 + co) * LANES
            w_b[co, c, :fcols] = ws_f[:, at:at + LANES].astype(BF16)
            w_b[co, c, LANES:LANES + fcols] = wn_f[:, at:at + LANES].astype(BF16)
    w_copy = pltpu.make_async_remote_copy(
        w_b.at[1 - core], w_p, q_ss.at[0], q_rs.at[0], device_id=(me, mate), device_id_type=MESH
    )
    w_copy.start()
    get_tiles.wait()
    tiles_f[...] = tiles_i[...].astype(F32)
    n_slots = tiles_f.shape[0]
    for copy in small:
        copy.wait()
    col_blocks = adj.shape[1] // BLK

    def place(i, c):
        r = i // col_blocks
        q = i % col_blocks
        total = jnp.zeros((BLK, BLK), F32)
        for k in range(n_slots):
            on = (rows_s[k] == r) & (cols_s[k] == q) & (k < count_s[0])
            total = total + tiles_f[k] * jnp.where(on, 1.0, 0.0)
        adj[pl.ds(pl.multiple_of(r * BLK, BLK), BLK), pl.ds(pl.multiple_of(q * BLK, BLK), BLK)] = total.astype(BF16)
        return c

    lax.fori_loop(0, (targets // BLK) * col_blocks, place, 0)
    degree = jnp.sum(adj[...].astype(F32), axis=1, keepdims=True)
    scale = 1.0 / jnp.maximum(degree, 1.0)
    get_cot.wait()
    w_copy.wait_recv()

    pltpu.make_async_copy(rows_buf.at[pl.ds(0, NDP - 1)], rows_buf.at[pl.ds(0, NDP - 1)], rows_rs).wait()
    sampled = rows_buf[...].reshape(NDP * TILE, fcols)
    self_rows = sampled[:targets]
    neigh = dot(adj[...], sampled) * scale
    x_b[0, :, :fcols] = self_rows
    x_b[1, :, :fcols] = neigh.astype(BF16)
    x_copy = pltpu.make_async_remote_copy(
        x_b, x_p, q_ss.at[1], q_rs.at[1], device_id=(me, mate), device_id_type=MESH
    )
    x_copy.start()

    both = jnp.concatenate([x_b[0], x_b[1]], axis=1)
    for k in CHIPS + (0,):
        chip = (x + k) % NX
        q_own[chip] = dot(both, w_b[core, chip])
    x_copy.wait_recv()
    other = jnp.concatenate([x_p[0], x_p[1]], axis=1)
    half = targets // HALVES
    for h in range(HALVES):
        low = h * half
        for k in CHIPS:
            chip = (x + k) % NX
            own = q_own[chip, low:low + half]
            p_send[h, chip] = (own + dot(other[low:low + half], w_p[chip])).astype(BF16)
            pltpu.make_async_remote_copy(
                p_send.at[h, chip], p_recv.at[h, x], send_sem.at[3 * CHUNKS + h], p_rs.at[h, x],
                device_id=(me, chip * 2 + core), device_id_type=MESH,
            ).start()
    preact = q_own[x] + dot(other, w_p[x]) + bias_v[...]

    xs_t = self_rows.astype(F32).T
    xn_t = neigh.T
    ones = jnp.where(lax.broadcasted_iota(jnp.int32, (TILE, targets), 0) == 0, 1.0, 0.0)
    xt_b[:fcols] = xs_t.astype(BF16)
    xt_b[fcols:fcols + TILE] = ones.astype(BF16)
    xt_b[fcols + TILE:] = xn_t.astype(BF16)

    def slope_copy(which, h, sem, to):
        return pltpu.make_async_remote_copy(
            sl_all.at[which, h], sl_all.at[which, h], sem, sl_rs.at[which, h],
            device_id=(me, to), device_id_type=MESH,
        )

    def activate(h):
        low = h * half
        total = preact[low:low + half]
        for k in (1, 3, 2):
            frm = (x + k) % NX
            pltpu.make_async_copy(p_recv.at[h, frm], p_recv.at[h, frm], p_rs.at[h, frm]).wait()
            total = total + p_recv[h, frm].astype(F32)
        row = low + lax.broadcasted_iota(jnp.int32, (half, LANES), 0)
        alive = jnp.where(row < seed_s[0], 1.0, 0.0)
        sigma = jax.nn.sigmoid(total)
        slope = cot_v[low:low + half].astype(F32) * alive * sigma * (1.0 + total * (1.0 - sigma))
        sl_all[feat, h] = slope.astype(BF16)
        for k in CHIPS:
            slope_copy(feat, h, send_sem.at[3 * CHUNKS + HALVES + h], (x + k) % NX * 2 + core).start()
        slope_copy(feat, h, f_ss.at[0, h], mate).start()
        hid_v[low:low + half] = (total * sigma * alive).astype(BF16)

    for h in range(HALVES):
        activate(h)
    put_hidden = pltpu.make_async_copy(hid_v, hidden_hbm, out_sem.at[0])
    put_hidden.start()

    def line(across, k):
        if across:
            return dp_of((y + k) % NY, z)
        return dp_of(y, (z + k) % NZ)

    class Chunk:
        def __init__(self, n):
            self.low, self.high, self.across = CHUNK_ROWS[n]
            self.send, self.recv, self.own, self.second, self.total = pieces[5 * n:5 * n + 5]
            self.here, self.there = (y, z) if self.across else (z, y)
            self.n = n
            base = 0 if self.low < s_rows else s_rows
            self.out = (n_hbm if self.across else s_hbm).at[:, pl.ds(self.low - base, self.high - self.low)]

        def first(self, at, grad):
            part = grad[self.low:self.high]

            @pl.when(at == self.here)
            def _():
                self.own[...] = part

            @pl.when(at != self.here)
            def _():
                self.send[at] = part.astype(BF16)
                to = dp_of(at, z) if self.across else dp_of(y, at)
                pltpu.make_async_remote_copy(
                    self.send.at[at], self.recv.at[self.here], send_sem.at[self.n], first_rs.at[self.n, self.here],
                    device_id=(to, feat), device_id_type=MESH,
                ).start()

        def add_first(self):
            total = self.own[...]
            for k in RING:
                frm = (self.here - k + NZ) % NZ
                pltpu.make_async_copy(self.recv.at[frm], self.recv.at[frm], first_rs.at[self.n, frm]).wait()
                total = total + self.recv[frm].astype(F32)
            self.second[self.there] = total.astype(BF16)
            for k in RING:
                pltpu.make_async_remote_copy(
                    self.second.at[self.there], self.second.at[self.there],
                    send_sem.at[CHUNKS + self.n], second_rs.at[self.n, self.there],
                    device_id=(line(not self.across, k), feat), device_id_type=MESH,
                ).start()

        def add_second(self):
            for k in RING:
                frm = (self.there - k + NZ) % NZ
                pltpu.make_async_copy(self.second.at[frm], self.second.at[frm], second_rs.at[self.n, frm]).wait()
            total = self.second[0].astype(F32)
            for n in range(1, NZ):
                total = total + self.second[n].astype(F32)
            self.total[...] = total.astype(BF16)
            for k in RING:
                pltpu.make_async_remote_copy(
                    self.total, self.out.at[self.here], send_sem.at[2 * CHUNKS + self.n], third_rs.at[self.n, self.here],
                    device_id=(line(self.across, k), feat), device_id_type=MESH,
                ).start()
            self.keep().start()

        def keep(self):
            return pltpu.make_async_copy(self.total, self.out.at[self.here], out_sem.at[1 + self.n])

        def finish(self):
            for k in RING:
                frm = (self.here - k + NZ) % NZ
                pltpu.make_async_copy(self.out.at[frm], self.out.at[frm], third_rs.at[self.n, frm]).wait()
            self.keep().wait()

    s_rows = fcols + TILE
    chunks = [Chunk(n) for n in range(CHUNKS)]

    def first(block):
        grad = dot(xt_b[...], sl_all[block].reshape(targets, LANES))
        for chunk in chunks:
            chunk.first(block // 2 + block % 2 * NX, grad)

    def wait_slope(which, h):
        pltpu.make_async_copy(sl_all.at[which, h], sl_all.at[which, h], sl_rs.at[which, h]).wait()

    first(feat)
    for h in range(HALVES):
        wait_slope(mate, h)
    first(mate)
    for group in ((1, 3), (2,)):
        for k in group:
            direct = (x + k) % NX * 2 + core
            for h in range(HALVES):
                wait_slope(direct, h)
                slope_copy(direct, h, f_ss.at[k, h], mate).start()
        for k in group:
            first((x + k) % NX * 2 + core)
        for k in group:
            passed = (x + k) % NX * 2 + 1 - core
            for h in range(HALVES):
                wait_slope(passed, h)
            first(passed)

    for chunk in chunks:
        chunk.add_first()
    for chunk in chunks:
        chunk.add_second()
    put_hidden.wait()

    def sent(buf, count, sem):
        pltpu.make_async_copy(buf.at[pl.ds(0, count)], buf.at[pl.ds(0, count)], sem).wait()

    sent(ids_y, NY - 1, ids_ss.at[0])
    sent(ids_buf, NZ - 1, ids_ss.at[1])
    sent(rows_send, NDP - 1, rows_ss)
    for h in range(HALVES):
        sent(p_send.at[h], NX - 1, send_sem.at[3 * CHUNKS + h])
        sent(p_send.at[h], NX - 1, send_sem.at[3 * CHUNKS + HALVES + h])
    for chunk in chunks:
        sent(chunk.send, NZ - 1, send_sem.at[chunk.n])
        sent(chunk.second, NZ - 1, send_sem.at[CHUNKS + chunk.n])
    w_copy.wait_send()
    x_copy.wait_send()
    for c in range(NX):
        for h in range(HALVES):
            pltpu.make_async_copy(sl_all.at[c, h], sl_all.at[c, h], f_ss.at[c, h]).wait()
    for chunk in chunks:
        chunk.finish()
    for chunk in chunks:
        sent(chunk.send, NZ - 1, send_sem.at[2 * CHUNKS + chunk.n])


def finish(
    hidden_in, s_in, n_in, hidden_ref, gself_ref, gneigh_ref, gbias_ref, h_v, s_v, n_v, gs_v, gn_v, gb_v, in_sem, out_sem
):
    fcols = gs_v.shape[0]
    gets = []
    for n, (src, dst) in enumerate(((s_in, s_v), (n_in, n_v))):
        for part in range(2):
            rows = pl.ds(part * NX, NX)
            gets.append(pltpu.make_async_copy(src.at[rows], dst.at[rows], in_sem.at[n * 2 + part]))
    for copy in gets:
        copy.start()
    get_hidden = pltpu.make_async_copy(hidden_in, h_v, in_sem.at[4])
    get_hidden.start()
    puts = []

    def put(src, dst):
        puts.append(pltpu.make_async_copy(src, dst, out_sem.at[len(puts)]))
        puts[-1].start()

    feat = lax.axis_index("feat")
    for src, dst, base, out in ((s_v, gs_v, 0, gself_ref), (n_v, gn_v, 2, gneigh_ref)):
        for part in range(2):
            gets[base + part].wait()
            for t in range(part * NX, part * NX + NX):
                c = (t % NX) * 2 + t // NX
                dst[:, c * LANES:(c + 1) * LANES] = src[t][:fcols].astype(F32)
        if base == 0:
            gb_v[...] = s_v[feat // 2 + feat % 2 * NX][fcols:fcols + TILE].astype(F32)[:1]
            put(gb_v, gbias_ref)
        put(dst, out)
        if base == 0:
            get_hidden.wait()
            put(h_v, hidden_ref)
    for copy in puts:
        copy.wait()


def on_device(table, node_ids, tiles, tile_rows, tile_cols, tile_count, seed_count, w_self, w_neigh, bias, cotangent):
    fcols = table.shape[1]
    hidden_all = w_self.shape[1]
    targets, hid = cotangent.shape
    s_rows, n_rows = fcols + TILE, fcols
    vmem = pltpu.VMEM
    dma = pltpu.SemaphoreType.DMA
    hbm = pl.BlockSpec(memory_space=pl.ANY)
    scratch = [
        vmem(table.shape[::-1], F32),
        vmem(table.shape[::-1], BF16),
        vmem(tiles.shape, jnp.int32),
        vmem(tiles.shape, F32),
        vmem(w_self.shape, F32),
        vmem(w_neigh.shape, F32),
        vmem((2, NX, 2 * LANES, LANES), BF16),
        vmem((NX, 2 * LANES, LANES), BF16),
        vmem(cotangent.shape, BF16),
        vmem((1, hid), F32),
        pltpu.SMEM(tile_rows.shape, jnp.int32),
        pltpu.SMEM(tile_cols.shape, jnp.int32),
        pltpu.SMEM(tile_count.shape, jnp.int32),
        pltpu.SMEM(seed_count.shape, jnp.int32),
        vmem((NY, 1, LANES), jnp.int32),
        vmem((NY, 1, LANES), jnp.int32),
        vmem((NZ, NY, 1, LANES), jnp.int32),
        vmem((NDP, TILE, fcols), BF16),
        vmem((NDP, TILE, fcols), BF16),
        vmem((targets, NDP * TILE), BF16),
        vmem((2, targets, LANES), BF16),
        vmem((2, targets, LANES), BF16),
        vmem((s_rows + n_rows, targets), BF16),
        vmem((NX, targets, hid), F32),
        vmem((HALVES, NX, targets // HALVES, hid), BF16),
        vmem((HALVES, NX, targets // HALVES, hid), BF16),
        vmem((NF, HALVES, targets // HALVES, hid), BF16),
        vmem((targets, hid), BF16),
    ]
    for low, high, _ in CHUNK_ROWS:
        rows = high - low
        scratch += [
            vmem((NZ, rows, LANES), BF16),
            vmem((NZ, rows, LANES), BF16),
            vmem((rows, LANES), F32),
            vmem((NZ, rows, LANES), BF16),
            vmem((rows, LANES), BF16),
        ]
    scratch += [
        dma((11,)),
        dma((2,)), dma, dma, dma, dma,
        dma((2,)), dma((2,)), dma((NX, HALVES)),
        dma((3 * CHUNKS + 2 * HALVES,)),
        dma((HALVES, NX)), dma((NF, HALVES)),
        dma((CHUNKS, NZ)), dma((CHUNKS, NZ)), dma((CHUNKS, NZ)),
        dma((1 + CHUNKS,)),
    ]
    hidden, s4, n4 = pl.pallas_call(
        kernel,
        out_shape=(
            jax.ShapeDtypeStruct((targets, hid), BF16),
            jax.ShapeDtypeStruct((NZ, s_rows, LANES), BF16),
            jax.ShapeDtypeStruct((NY, n_rows, LANES), BF16),
        ),
        in_specs=[hbm] * 11,
        out_specs=(hbm,) * 3,
        scratch_shapes=scratch,
        compiler_params=pltpu.CompilerParams(
            collective_id=0, has_side_effects=True, vmem_limit_bytes=VMEM_LIMIT
        ),
        cost_estimate=pl.CostEstimate(flops=300_000_000, bytes_accessed=4_000_000, transcendentals=65536),
    )(
        table.T, node_ids.reshape(NY, 1, NZ * TILE), tiles, tile_rows, tile_cols,
        tile_count, seed_count, w_self, w_neigh, bias.reshape(1, hid), cotangent,
    )
    hidden, grad_self, grad_neigh, grad_bias = pl.pallas_call(
        finish,
        out_shape=(
            jax.ShapeDtypeStruct((targets, hid), BF16),
            jax.ShapeDtypeStruct(w_self.shape, F32),
            jax.ShapeDtypeStruct(w_neigh.shape, F32),
            jax.ShapeDtypeStruct((1, hid), F32),
        ),
        in_specs=[hbm] * 3,
        out_specs=(hbm,) * 4,
        scratch_shapes=[
            vmem((targets, hid), BF16), vmem((NZ, s_rows, LANES), BF16), vmem((NY, n_rows, LANES), BF16),
            vmem(w_self.shape, F32), vmem(w_neigh.shape, F32), vmem((1, hid), F32), dma((5,)), dma((4,)),
        ],
    )(hidden, s4, n4)
    return hidden, grad_self, grad_neigh, grad_bias.reshape(hid)


def solution(mesh):
    placed = (
        P("dp", "feat"),
        P("dp"),
        P("dp", None, None),
        P("dp"),
        P("dp"),
        P("dp"),
        P("dp"),
        P("feat", None),
        P("feat", None),
        P("feat"),
        P("dp", "feat"),
    )
    return jax.shard_map(
        on_device,
        mesh=mesh,
        in_specs=placed,
        out_specs=(P("dp", "feat"), P("feat", None), P("feat", None), P("feat")),
        check_vma=False,
    )
```
